32 devices in a mesh: blk: 4 (over x, core), wide: 8 (over z, y).
Axes of the slice: x: 2, y: 2, z: 4, core: 2. Of those that a mesh axis runs over, the one named last changes fastest.
Arguments:
- observed: bfloat16 [8192, 5120], P(('blk', 'wide')), may hold values from -8 to 8
- mask_bits: int32 [8192, 640], P(('blk', 'wide')), may hold values from 0 to 255, as said below
- frame_factors: float32 [8192, 256], P(('blk', 'wide')), may hold values from -2 to 2
- pixel_factors: bfloat16 [32768, 256], P(('blk', 'wide')), may hold values from -2 to 2
Outputs:
- frames_out: float32 [8192, 256], P(('blk', 'wide'))
- pixels_out: bfloat16 [32768, 256], P(('blk', 'wide'))
The draws below stay inside these ranges and needn't reach their ends.
Inputs may be any that keep to these rules, and one draw needn't show every extreme that they name: `mask_bits`: each word holds 8 independent flags, each set with probability one half.
All inputs are finite; a program needn't handle non-finite values.
Results may differ from the reference program's by a relative error of at most 0.0071.
Values may be sent and summed in bfloat16 or wider, within the bound.
No kernel may reach another device: no remote copies, remote signals or barrier semaphores. Data moves between devices by JAX's collectives and lax.ppermute only.
A program may use at most 64 MiB of HBM per device.

```python
from functools import partial
import jax
import jax.numpy as jnp
from jax import lax

RANK = 256
PB = 1024
VISITS = 5
FR_DEV = 256
FRAMES = 8192
PIXELS = 32768
WORDS = 640
N_BLK = 4
N_WIDE = 8


def draw_mask_bits(key, part):
    values = jax.random.randint(key, (FRAMES, WORDS), 0, 256, dtype=jnp.int32)
    values = values.at[0, 0].set(255)
    return values.at[0, 1].set(0)


def shard_levels(stream_key, extent, shards, smallest, high):
    def one(position, shards_of):
        draws = jax.random.uniform(jax.random.fold_in(jax.random.fold_in(stream_key, 6), position), (shards_of,), jnp.float32, smallest / len(shards), high / len(shards))
        return jnp.repeat(jnp.exp(draws), extent[position] // shards_of).reshape((-1,) + (1,) * (len(extent) - position - 1))

    loudness = one(*shards[0])
    for cut in shards[1:]:
        loudness = loudness * one(*cut)
    return loudness


def scatter_about(own_key, shape, width, reach, split=(), held_as=jnp.bfloat16):
    drawn = width * jax.random.normal(own_key, shape, jnp.float32)
    if split:
        drawn = drawn * shard_levels(own_key, shape, split, -0.22, 0.18)
    return jnp.clip(drawn, -reach, reach).astype(held_as)


def setup_inputs(seed: int = 0) -> dict:
    streams_of = jax.random.split(jax.random.key(seed), 5)
    return {
        "observed": scatter_about(streams_of[0], (FRAMES, VISITS * PB), 1.5, 8.0, ((0, 32),)),
        "mask_bits": draw_mask_bits(jax.random.fold_in(streams_of[4], 71), 0),
        "frame_factors": scatter_about(streams_of[2], (FRAMES, RANK), 0.25, 2.0, ((0, 32),), jnp.float32),
        "pixel_factors": scatter_about(streams_of[3], (PIXELS, RANK), 0.25, 2.0, ((0, 32),)),
    }


clip_level = 1.0
step_frames = 0.01
step_pixels = 0.02
decay_weight = 0.1


def unpack_mask(packed):
    shifts = jnp.arange(8, dtype=jnp.int32)
    expanded = jnp.bitwise_and(jnp.right_shift(packed[..., None, :], shifts[:, None]), 1)
    return expanded.reshape(packed.shape[:-1] + (8 * packed.shape[-1],)).astype(jnp.float32)


def tile_update(visit_index, operands):
    observed_row, packed_row, frames_row, pixels_row = operands
    lower = visit_index * PB
    wanted = observed_row[..., lower:lower + PB].astype(jnp.float32)
    visible = unpack_mask(packed_row)[..., lower:lower + PB]
    frames_low = lax.optimization_barrier(frames_row.astype(jnp.bfloat16)).astype(jnp.float32)
    pixels_wide = pixels_row.astype(jnp.float32)
    predicted = jnp.einsum('wfr,wpr->wfp', frames_low, pixels_wide)
    errors = visible * (wanted - predicted)
    weights = clip_level / jnp.maximum(jnp.abs(errors), clip_level)
    scaled = lax.optimization_barrier((weights * errors).astype(jnp.bfloat16)).astype(jnp.float32)
    grad_frames = jnp.einsum('wfp,wpr->wfr', scaled, pixels_wide)
    grad_pixels = jnp.einsum('wfp,wfr->wpr', scaled, frames_low)
    new_frames = frames_row + step_frames * (grad_frames - decay_weight * frames_row)
    new_pixels = (pixels_wide + step_pixels * (grad_pixels - decay_weight * pixels_wide)).astype(jnp.bfloat16)
    return new_frames, new_pixels


def reference(observed, mask_bits, frame_factors, pixel_factors):
    grid_obs = observed.reshape(N_BLK, N_WIDE, FR_DEV, VISITS * PB)
    grid_bits = mask_bits.reshape(N_BLK, N_WIDE, FR_DEV, WORDS)
    frames = frame_factors.reshape(N_BLK, N_WIDE, FR_DEV, RANK)
    pixels = pixel_factors.reshape(N_BLK, N_WIDE, PB, RANK)
    for visit_index in range(VISITS):
        frames, pixels = lax.map(partial(tile_update, visit_index), (grid_obs, grid_bits, frames, pixels))
        if visit_index < VISITS - 2:
            pixels = jnp.roll(pixels, 1, axis=0)
        elif visit_index == VISITS - 2:
            pixels = jnp.roll(pixels, 1, axis=1)
    return frames.reshape(FRAMES, RANK), pixels.reshape(PIXELS, RANK)
```

```python
import jax
import jax.numpy as jnp
from jax import lax
from jax.experimental import pallas as pl
from jax.experimental.pallas import tpu as pltpu
from jax.sharding import PartitionSpec as P

CHUNKS = 4

step_frames = 0.01
step_pixels = 0.02
decay_weight = 0.1

VMEM = pl.BlockSpec(memory_space=pltpu.VMEM)
HBM = pl.BlockSpec(memory_space=pltpu.HBM)


def shifted(value, axis):
    count = lax.axis_size(axis)
    return lax.ppermute(value, axis, [(s, (s + 1) % count) for s in range(count)])


def flags(bits, lower, count):
    words = bits.shape[1]
    pieces = []
    at = lower
    while at < lower + count:
        flag, word = divmod(at, words)
        size = min(words - word, lower + count - at)
        pieces.append(lax.shift_right_logical(bits[:, word : word + size], flag) & 1)
        at += size
    return pieces[0] if len(pieces) == 1 else jnp.concatenate(pieces, axis=1)


def tile(lower, first, frames, done, observed, bits, block):
    count = block.shape[0]
    frames_low = frames.astype(jnp.bfloat16)
    predicted = lax.dot_general(
        frames_low, block, (((1,), (1,)), ((), ())), preferred_element_type=jnp.float32
    )
    errors = observed[:, lower : lower + count].astype(jnp.float32) - predicted
    clipped = jnp.clip(errors, -1.0, 1.0)
    scaled = jnp.where(flags(bits, lower, count) != 0, clipped, 0.0).astype(jnp.bfloat16)
    grad_pixels = lax.dot_general(
        scaled, frames_low, (((0,), (0,)), ((), ())), preferred_element_type=jnp.float32
    )
    current = block.astype(jnp.float32)
    new = (current + step_pixels * (grad_pixels - decay_weight * current)).astype(jnp.bfloat16)
    grad_frames = jnp.dot(scaled, block, preferred_element_type=jnp.float32)
    if first:
        return new, frames + step_frames * (grad_frames - decay_weight * frames)
    return new, done + step_frames * grad_frames


def cost(observed, count, rank):
    return pl.CostEstimate(flops=0, bytes_accessed=0, transcendentals=0)


def params():
    return pltpu.CompilerParams(vmem_limit_bytes=24 * 1024 * 1024)


def load_kernel(width, size, observed, mask_bits, frames, pixels, observed_v, bits_v, pixels_v, state, new, sems):
    copies = [
        pltpu.make_async_copy(frames, state.at[0], sems.at[0]),
        pltpu.make_async_copy(pixels, pixels_v, sems.at[1]),
        pltpu.make_async_copy(mask_bits, bits_v, sems.at[2]),
        pltpu.make_async_copy(observed.at[:, :width], observed_v.at[:, :width], sems.at[3]),
    ]
    for copy in copies:
        copy.start()
    for copy in copies:
        copy.wait()
    new[...], state[1] = tile(0, True, state[0], None, observed_v, bits_v, pixels_v[:size])


def rest_kernel(width, chunk, size, observed, bits, pixels, state, observed_in, new, state_out, observed_v, sem):
    del observed_in
    copy = pltpu.make_async_copy(observed.at[:, width:], observed_v.at[:, width:], sem)
    copy.start()
    rows = slice(chunk * size, (chunk + 1) * size)
    new[...], state_out[1] = tile(
        chunk * size, False, state[0], state[1], observed_v, bits, pixels[rows]
    )
    copy.wait()


def step_kernel(lower, first, old, rows, observed, bits, block, state, new, state_out):
    new[...], state_out[1 - old] = tile(
        lower, first, state[old], None if first else state[1 - old], observed, bits, block[rows]
    )


def last_kernel(lower, first, last, old, at, size, observed, bits, block, state, pixels_in, *refs):
    del pixels_in
    if last:
        state_out, pixels_out, frames_out, held, sem, sem2 = refs
    else:
        state_out, pixels_out, held, sem = refs
    held[...], done = tile(
        lower, first, state[old], None if first else state[1 - old], observed, bits, block[...]
    )
    copy = pltpu.make_async_copy(held, pixels_out.at[at : at + size], sem)
    copy.start()
    state_out[1 - old] = done
    if last:
        copy2 = pltpu.make_async_copy(state_out.at[1 - old], frames_out, sem2)
        copy2.start()
        copy2.wait()
    copy.wait()


def struct(shape, dtype):
    return jax.ShapeDtypeStruct(shape, dtype)


def body(observed, mask_bits, frame_factors, pixel_factors):
    width, rank = pixel_factors.shape
    visits = observed.shape[1] // width
    size = width // CHUNKS
    chunk_shape = struct((size, rank), jnp.bfloat16)
    state_shape = struct((2,) + frame_factors.shape, jnp.float32)
    observed_shape = struct(observed.shape, observed.dtype)
    dma = pltpu.SemaphoreType.DMA

    def call(kernel, **kw):
        return pl.pallas_call(
            kernel, compiler_params=params(), cost_estimate=cost(observed, size, rank), **kw
        )

    def first_kernel(*refs):
        load_kernel(width, size, *refs)

    observed_v, bits, block, state, new = call(
        first_kernel,
        out_shape=(
            observed_shape,
            struct(mask_bits.shape, mask_bits.dtype),
            struct(pixel_factors.shape, pixel_factors.dtype),
            state_shape,
            chunk_shape,
        ),
        in_specs=[HBM] * 4,
        out_specs=(VMEM,) * 5,
        scratch_shapes=[dma((4,))],
    )(observed, mask_bits, frame_factors, pixel_factors)
    coming = [shifted(new, "blk")]

    def second_kernel(*refs):
        rest_kernel(width, 1, size, *refs)

    new, state, observed_v = call(
        second_kernel,
        out_shape=(chunk_shape, state_shape, observed_shape),
        in_specs=[HBM] + [VMEM] * 4,
        out_specs=(VMEM,) * 3,
        scratch_shapes=[dma],
        input_output_aliases={3: 1, 4: 2},
    )(observed, bits, block, state, observed_v)
    coming.append(shifted(new, "blk"))

    def step(visit, chunk, block, state, rows):
        def kernel(*refs):
            step_kernel(visit * width + chunk * size, chunk == 0, visit % 2, rows, *refs)

        return call(
            kernel,
            out_shape=(chunk_shape, state_shape),
            in_specs=[VMEM] * 4,
            out_specs=(VMEM,) * 2,
            input_output_aliases={3: 1},
        )(observed_v, bits, block, state)

    for c in range(2, CHUNKS):
        new, state = step(0, c, block, state, slice(c * size, (c + 1) * size))
        coming.append(shifted(new, "blk"))

    for visit in range(1, visits - 1):
        axis = "blk" if visit < visits - 2 else "wide"
        sent = []
        for c in range(CHUNKS):
            new, state = step(visit, c, coming[c], state, slice(None))
            sent.append(shifted(new, axis))
        coming = sent

    visit = visits - 1
    pixels_out = None
    for c in range(CHUNKS):
        last = c == CHUNKS - 1

        def kernel(*refs, c=c, last=last):
            if c == 0:
                refs = refs[:4] + (None,) + refs[4:]
            last_kernel(visit * width + c * size, c == 0, last, visit % 2, c * size, size, *refs)

        out_shape = [state_shape, struct(pixel_factors.shape, pixel_factors.dtype)]
        out_specs = [VMEM, HBM]
        scratch = [pltpu.VMEM((size, rank), jnp.bfloat16), dma]
        if last:
            out_shape.append(struct(frame_factors.shape, jnp.float32))
            out_specs.append(HBM)
            scratch.append(dma)
        args = [observed_v, bits, coming[c], state]
        specs = [VMEM] * 4
        aliases = {3: 0}
        if c:
            args.append(pixels_out)
            specs.append(HBM)
            aliases[4] = 1
        outs = call(
            kernel,
            out_shape=tuple(out_shape),
            in_specs=specs,
            out_specs=tuple(out_specs),
            scratch_shapes=scratch,
            input_output_aliases=aliases,
        )(*args)
        state, pixels_out = outs[:2]
    return outs[2], pixels_out


def solution(mesh):
    spec = P(("blk", "wide"), None)
    return jax.shard_map(
        body, mesh=mesh, in_specs=(spec,) * 4, out_specs=(spec, spec), check_vma=False
    )
```

```python
import jax
import jax.numpy as jnp
from jax import lax
from jax.experimental import pallas as pl
from jax.experimental.pallas import tpu as pltpu
from jax.sharding import PartitionSpec as P

VISITS = 5
CHUNKS = 2
PIECES = 2

step_frames = 0.01
step_pixels = 0.02
decay_weight = 0.1

VMEM = pl.BlockSpec(memory_space=pltpu.VMEM)
HBM = pl.BlockSpec(memory_space=pltpu.HBM)
DMA = pltpu.SemaphoreType.DMA


def over_chip(value):
    count = lax.axis_size("blk")
    return lax.ppermute(value, "blk", [(s, s + 1 - 2 * (s % 2)) for s in range(count)])


def to_next_pair(value):
    count = lax.axis_size("blk")
    return lax.ppermute(value, "blk", [(s, (s + 2) % count) for s in range(count)])


def to_next_wide(value):
    count = lax.axis_size("wide")
    return lax.ppermute(value, "wide", [(s, (s + 1) % count) for s in range(count)])


def my_core():
    return lax.axis_index("blk") % 2


def flags(bits, lower, count):
    words = bits.shape[1]
    pieces = []
    at = lower
    while at < lower + count:
        flag, word = divmod(at, words)
        size = min(words - word, lower + count - at)
        pieces.append(lax.shift_right_logical(bits[:, word : word + size], flag) & 1)
        at += size
    whole = pieces[0] if len(pieces) == 1 else jnp.concatenate(pieces, axis=1)
    return whole.astype(jnp.float32).astype(jnp.bfloat16)


def tile(frames, block, wanted, visible):
    frames_low = frames.astype(jnp.bfloat16)
    predicted = lax.dot_general(
        frames_low, block, (((1,), (1,)), ((), ())), preferred_element_type=jnp.float32
    )
    errors = wanted.astype(jnp.float32) - predicted
    scaled = jnp.clip(errors, -1.0, 1.0).astype(jnp.bfloat16) * visible
    grad_pixels = lax.dot_general(
        scaled, frames_low, (((0,), (0,)), ((), ())), preferred_element_type=jnp.float32
    )
    current = block.astype(jnp.float32)
    new = (current + step_pixels * (grad_pixels - decay_weight * current)).astype(jnp.bfloat16)
    return new, jnp.dot(scaled, block, preferred_element_type=jnp.float32)


def moved(frames, grad):
    return frames + step_frames * (grad - decay_weight * frames)


def struct(shape, dtype):
    return jax.ShapeDtypeStruct(shape, dtype)


def call(kernel, args, specs, outs, out_specs, scratch=(), aliases=None):
    return pl.pallas_call(
        kernel,
        out_shape=tuple(outs),
        in_specs=list(specs),
        out_specs=tuple(out_specs),
        scratch_shapes=list(scratch),
        input_output_aliases=aliases or {},
        compiler_params=pltpu.CompilerParams(vmem_limit_bytes=24 * 1024 * 1024),
        cost_estimate=pl.CostEstimate(flops=0, bytes_accessed=0, transcendentals=0),
    )(*args)


def body(observed, mask_bits, frame_factors, pixel_factors):
    width, rank = pixel_factors.shape
    rows = frame_factors.shape[0]
    half = width // 2
    size = half // CHUNKS
    later = VISITS - 1
    low = jnp.bfloat16
    chunk_t = struct((size, rank), low)
    frames_t = struct((rows, rank), jnp.float32)
    both_t = struct((2, rows, rank), jnp.float32)
    observed, mask_bits, frame_factors, pixel_factors = (
        pltpu.with_memory_space_constraint(a, pltpu.HBM)
        for a in (observed, mask_bits, frame_factors, pixel_factors)
    )

    def own_tile(give, c, observed0, bits, pixels, frames, visible):
        for core in range(2):
            mine = 1 - core if give else core

            @pl.when(my_core() == core)
            def _(lower=mine * half + c * size):
                visible[...] = flags(bits, lower, size)

        mine = 1 - my_core() if give else my_core()
        at = pl.multiple_of(mine * half + c * size, size)
        return tile(frames, pixels[pl.ds(at, size), :], observed0[:, pl.ds(at, size)], visible[...])

    def load_kernel(observed, mask_bits, frames, pixels, observed0, bits, pixels_v, state, new, visible, sems):
        copies = [
            pltpu.make_async_copy(frames, state.at[0], sems.at[0]),
            pltpu.make_async_copy(pixels, pixels_v, sems.at[1]),
            pltpu.make_async_copy(mask_bits, bits, sems.at[2]),
            pltpu.make_async_copy(observed.at[:, :width], observed0, sems.at[3]),
        ]
        for copy in copies:
            copy.start()
        for copy in copies:
            copy.wait()
        new[...], grad = own_tile(True, 0, observed0, bits, pixels_v, state[0], visible)
        state[1] = moved(state[0], grad)

    observed0, bits, pixels_v, state, new = call(
        load_kernel,
        (observed, mask_bits, frame_factors, pixel_factors),
        [HBM] * 4,
        (
            struct((rows, width), low),
            struct(mask_bits.shape, mask_bits.dtype),
            struct(pixel_factors.shape, low),
            both_t,
            chunk_t,
        ),
        [VMEM] * 5,
        scratch=[pltpu.VMEM((rows, size), low), DMA((4,))],
    )

    def own_step(give, c, state, last=False):
        def kernel(observed0, bits, pixels, state, new, state_out, *rest):
            frames = state[0]
            new[...], grad = own_tile(give, c, observed0, bits, pixels, frames, rest[-1])
            done = state[1] + step_frames * grad
            state_out[0] = frames
            state_out[1] = done
            if last:
                rest[0][...] = done

        outs = [chunk_t, both_t] + ([frames_t] if last else [])
        return call(
            kernel,
            (observed0, bits, pixels_v, state),
            [VMEM] * 4,
            outs,
            [VMEM] * len(outs),
            scratch=[pltpu.VMEM((rows, size), low)],
            aliases={3: 1},
        )

    def route(got, kept):
        def kernel(got, kept, out):
            out[...] = jnp.where(my_core() == 0, got[...], kept[...])

        return call(kernel, (got, kept), [VMEM] * 2, [chunk_t], [VMEM])[0]

    got, kept, first_sent = [], [], []
    for c in range(CHUNKS):
        if c:
            new, state = own_step(True, c, state)
        got.append(over_chip(new))
        last = c == CHUNKS - 1
        outs = own_step(False, c, state, last)
        kept.append(outs[0])
        state = outs[1]
        routed = route(got[c], kept[c])
        first_sent.append(to_next_pair(routed))
    own = outs[2]
    other = over_chip(own)

    def share_kernel(observed, bits, after, observed_own, visible_own, share1, share, sems):
        del after
        core_here = my_core()
        copies = []
        for v in range(later):
            for n, (mine, target) in enumerate(
                (
                    (core_here, observed_own.at[:, v * half : (v + 1) * half]),
                    (1 - core_here, share1.at[:rows] if v == 0 else share.at[v - 1, :rows]),
                )
            ):
                at = pl.multiple_of((v + 1) * width + mine * half, half)
                copies.append(
                    pltpu.make_async_copy(observed.at[:, pl.ds(at, half)], target, sems.at[v, n])
                )
        for copy in copies:
            copy.start()
        for core in range(2):

            @pl.when(my_core() == core)
            def _(core=core):
                for v in range(later):
                    at = (v + 1) * width
                    visible_own[:, v * half : (v + 1) * half] = flags(bits, at + core * half, half)
                    theirs = flags(bits, at + (1 - core) * half, half)
                    if v == 0:
                        share1[rows:] = theirs
                    else:
                        share[v - 1, rows:] = theirs

        for copy in copies:
            copy.wait()

    own_t = struct((rows, later * half), low)
    observed_own, visible_own, share1, share = call(
        share_kernel,
        (observed, bits, routed),
        [HBM, VMEM, VMEM],
        (own_t, own_t, struct((2 * rows, half), low), struct((later - 1, 2 * rows, half), low)),
        [VMEM] * 4,
        scratch=[DMA((later, 2))],
    )
    share1 = over_chip(share1)
    share = over_chip(share)

    def operand(idx, v, c, observed_own, visible_own, share1, share):
        at = (v - 1) * half + c * size
        cols = slice(c * size, (c + 1) * size)
        theirs = share1 if v == 1 else share.at[v - 2]
        here = my_core() == idx
        wanted = jnp.where(here, observed_own[:, at : at + size], theirs[:rows, cols])
        visible = jnp.where(here, visible_own[:, at : at + size], theirs[rows:, cols])
        return wanted, visible

    def stage(c, even, odd, block, state, part, sums, update=(), extra=None):
        visited = [(idx, v) for idx, v in ((0, even), (1, odd)) if v is not None]
        last = c == CHUNKS - 1
        n_sums = len(sums)
        piece = len(visited) * rows // PIECES

        def kernel(observed_own, visible_own, share1, share, block, state, part, *refs):
            got = refs[:n_sums]
            outs = refs[n_sums:]
            new, state_out, part_out = outs[:3]
            frames = [state[0], state[1]]
            grads = [part[0], part[1]]
            if got:
                total = jnp.concatenate([g[...] for g in got], axis=0).astype(jnp.float32)
                for n, idx in enumerate(update):
                    frames[idx] = moved(frames[idx], grads[idx] + total[n * rows : (n + 1) * rows])
            held = block[...]
            for idx, v in visited:
                held, grad = tile(
                    frames[idx], held, *operand(idx, v, c, observed_own, visible_own, share1, share)
                )
                grads[idx] = grad if c == 0 else grads[idx] + grad
            new[...] = held
            for idx in range(2):
                state_out[idx] = frames[idx]
                part_out[idx] = grads[idx]
            if last:
                sent = jnp.concatenate([grads[idx].astype(low) for idx, _ in visited], axis=0)
                for n in range(PIECES):
                    outs[3 + n][...] = sent[n * piece : (n + 1) * piece]

        outs = [chunk_t, both_t, both_t]
        if last:
            outs += [struct((piece, rank), low)] * PIECES
        return call(
            kernel,
            (observed_own, visible_own, share1, share, block, state, part, *sums),
            [VMEM] * (7 + n_sums),
            outs,
            [VMEM] * len(outs),
            aliases={5: 1, 6: 2},
        )

    def pair_kernel(c, observed_own, visible_own, share1, share, got, kept, own, other, part, new, state, part_out, *sent):
        first = my_core() == 0
        frames = jnp.where(first, other[...], own[...])
        if c == 0:
            state[0] = jnp.where(first, own[...], other[...])
            state[1] = frames
        block = jnp.where(first, kept[...], got[...])
        new[...], grad = tile(frames, block, *operand(1, 1, c, observed_own, visible_own, share1, share))
        if c:
            grad = grad + part[1]
        part_out[1] = grad
        if sent:
            sent[0][...] = grad.astype(low)

    second_sent, sums = [], []
    part = None
    for c in range(CHUNKS):
        last = c == CHUNKS - 1

        def kernel(*refs, c=c):
            refs = list(refs)
            if c == 0:
                refs.insert(8, None)
            else:
                refs.insert(10, None)
            pair_kernel(c, *refs)

        args = [observed_own, visible_own, share1, share, got[c], kept[c], own, other]
        outs = [chunk_t, both_t, both_t]
        if c:
            args.append(part)
            outs = [chunk_t, both_t]
        if last:
            outs.append(struct((rows, rank), low))
        outs = call(kernel, args, [VMEM] * len(args), outs, [VMEM] * len(outs))
        second_sent.append(to_next_pair(outs[0]))
        if c == 0:
            state, part = outs[1:3]
        else:
            part = outs[1]
        if last:
            sums = [over_chip(outs[-1])]

    def stages(even, odd, blocks, state, part, sums, update, send):
        sent = []
        for c in range(CHUNKS):
            outs = stage(c, even, odd, blocks[c], state, part, sums if c == 0 else (), update)
            sent.append(send(outs[0]))
            state, part = outs[1:3]
        return sent, state, part, [over_chip(s) for s in outs[3:]]

    third_sent, state, part, sums = stages(1, 2, first_sent, state, part, sums, (1,), to_next_pair)
    odd_sent, state, part, sums = stages(2, 3, second_sent, state, part, sums, (0, 1), to_next_wide)
    even_sent, state, part, sums = stages(3, None, third_sent, state, part, sums, (0, 1), to_next_wide)

    odd_done = []
    for c in range(CHUNKS):
        outs = stage(c, None, 4, odd_sent[c], state, part, ())
        odd_done.append(outs[0])
        state, part = outs[1:3]

    mine, theirs = [], []
    for c in range(CHUNKS):
        last = c == CHUNKS - 1
        n_sums = len(sums) if c == 0 else 0

        def kernel(observed_own, visible_own, share1, share, block, state, part, done, *refs, c=c, last=last):
            got, outs = refs[:n_sums], refs[n_sums:]
            frames, grad = state[0], part[0]
            if got:
                total = jnp.concatenate([g[...] for g in got], axis=0).astype(jnp.float32)
                frames = moved(frames, grad + total)
            new, step = tile(
                frames, block[...], *operand(0, 4, c, observed_own, visible_own, share1, share)
            )
            grad = step if c == 0 else grad + step
            first = my_core() == 0
            outs[0][...] = jnp.where(first, new, done[...])
            outs[1][...] = jnp.where(first, done[...], new)
            outs[2][0] = frames
            outs[2][1] = state[1]
            outs[3][0] = grad
            outs[3][1] = part[1]
            if last:
                outs[4][...] = jnp.where(first, part[1], grad).astype(low)

        outs = [chunk_t, chunk_t, both_t, both_t]
        if last:
            outs.append(struct((rows, rank), low))
        args = [observed_own, visible_own, share1, share, even_sent[c], state, part, odd_done[c]]
        args += sums if c == 0 else []
        outs = call(kernel, args, [VMEM] * len(args), outs, [VMEM] * len(outs), aliases={5: 2, 6: 3})
        mine.append(outs[0])
        theirs.append(over_chip(outs[1]))
        state, part = outs[2:4]
    total = over_chip(outs[4])

    def write_kernel(*refs):
        mine, theirs = refs[:CHUNKS], refs[CHUNKS : 2 * CHUNKS]
        state, part, total, frames_out, pixels_out, frames, sems = refs[2 * CHUNKS :]
        core = my_core()
        copies = []
        for c in range(CHUNKS):
            for n, (source, at) in enumerate(((mine[c], core), (theirs[c], 1 - core))):
                to = pl.multiple_of(at * half + c * size, size)
                copies.append(
                    pltpu.make_async_copy(source, pixels_out.at[pl.ds(to, size)], sems.at[c, n])
                )
        for copy in copies:
            copy.start()
        first = core == 0
        frames[...] = moved(
            jnp.where(first, state[0], state[1]),
            jnp.where(first, part[0], part[1]) + total[...].astype(jnp.float32),
        )
        copy = pltpu.make_async_copy(frames, frames_out, sems.at[CHUNKS, 0])
        copy.start()
        for one in copies:
            one.wait()
        copy.wait()

    return call(
        write_kernel,
        (*mine, *theirs, state, part, total),
        [VMEM] * (2 * CHUNKS + 3),
        (frames_t, struct(pixel_factors.shape, low)),
        [HBM] * 2,
        scratch=[pltpu.VMEM((rows, rank), jnp.float32), DMA((CHUNKS + 1, 2))],
    )


def solution(mesh):
    spec = P(("blk", "wide"), None)
    return jax.shard_map(
        body, mesh=mesh, in_specs=(spec,) * 4, out_specs=(spec, spec), check_vma=False
    )
```

```python
import jax
import jax.numpy as jnp
from jax import lax
from jax.experimental import pallas as pl
from jax.experimental.pallas import tpu as pltpu
from jax.sharding import PartitionSpec as P

CHUNKS = 4
LAST_FLOPS = 200_000_000

step_frames = 0.01
step_pixels = 0.02
decay_weight = 0.1

LOW = jnp.bfloat16
VMEM = pl.BlockSpec(memory_space=pltpu.VMEM)
HBM = pl.BlockSpec(memory_space=pltpu.HBM)
DMA = pltpu.SemaphoreType.DMA


def shifted(value, axis):
    count = lax.axis_size(axis)
    return lax.ppermute(value, axis, [(s, (s + 1) % count) for s in range(count)])


def struct(shape, dtype=LOW):
    return jax.ShapeDtypeStruct(shape, dtype)


def call(name, kernel, args, outs, in_specs=None, out_specs=None, scratch=(), aliases=None, flops=0):
    return pl.pallas_call(
        kernel,
        name=name,
        out_shape=tuple(outs),
        in_specs=in_specs or [VMEM] * len(args),
        out_specs=tuple(out_specs or [VMEM] * len(outs)),
        scratch_shapes=list(scratch),
        input_output_aliases=aliases or {},
        compiler_params=pltpu.CompilerParams(vmem_limit_bytes=24 * 1024 * 1024),
        cost_estimate=pl.CostEstimate(flops=flops, bytes_accessed=0, transcendentals=0),
    )(*args)


def flags(bits, lower, count):
    words = bits.shape[1]
    pieces = []
    at = lower
    while at < lower + count:
        flag, word = divmod(at, words)
        size = min(words - word, lower + count - at)
        pieces.append(lax.shift_right_logical(bits[:, word : word + size], flag) & 1)
        at += size
    return pieces[0] if len(pieces) == 1 else jnp.concatenate(pieces, axis=1)


def tile(frames, block, wanted, visible):
    frames_low = frames.astype(LOW)
    predicted = lax.dot_general(
        frames_low, block, (((1,), (1,)), ((), ())), preferred_element_type=jnp.float32
    )
    errors = wanted.astype(jnp.float32) - predicted
    clipped = jnp.clip(errors, -1.0, 1.0)
    scaled = jnp.where(visible != 0, clipped, 0.0).astype(LOW)
    grad_pixels = lax.dot_general(
        scaled, frames_low, (((0,), (0,)), ((), ())), preferred_element_type=jnp.float32
    )
    current = block.astype(jnp.float32)
    new = (current + step_pixels * (grad_pixels - decay_weight * current)).astype(LOW)
    return new, jnp.dot(scaled, block, preferred_element_type=jnp.float32)


def added(frames, done, grad):
    if done is None:
        return frames + step_frames * (grad - decay_weight * frames)
    return done + step_frames * grad


def body(observed, mask_bits, frame_factors, pixel_factors):
    width, rank = pixel_factors.shape
    rows = frame_factors.shape[0]
    visits = observed.shape[1] // width
    size = width // CHUNKS
    chunk_t = struct((size, rank))
    frames_t = struct((rows, rank), jnp.float32)
    whole = observed
    observed, mask_bits, frame_factors, pixel_factors = (
        pltpu.with_memory_space_constraint(a, pltpu.HBM)
        for a in (observed, mask_bits, frame_factors, pixel_factors)
    )

    def load_kernel(observed, mask_bits, frames_in, pixels_in, observed0, bits, pixels, frames, new, done, sems):
        first = [
            pltpu.make_async_copy(mask_bits.at[:, :size], bits.at[:, :size], sems.at[0]),
            pltpu.make_async_copy(pixels_in.at[:size], pixels.at[:size], sems.at[1]),
            pltpu.make_async_copy(observed.at[:, :size], observed0.at[:, :size], sems.at[2]),
            pltpu.make_async_copy(frames_in, frames, sems.at[3]),
        ]
        rest = [
            pltpu.make_async_copy(pixels_in.at[size:], pixels.at[size:], sems.at[4]),
            pltpu.make_async_copy(observed.at[:, size:width], observed0.at[:, size:], sems.at[5]),
            pltpu.make_async_copy(mask_bits.at[:, size:], bits.at[:, size:], sems.at[6]),
        ]
        for copy in first + rest:
            copy.start()
        for copy in first:
            copy.wait()
        new[...], grad = tile(frames[...], pixels[:size], observed0[:, :size], flags(bits, 0, size))
        done[...] = added(frames[...], None, grad)
        for copy in rest:
            copy.wait()

    observed0, bits, pixels, frames, new, done = call(
        "load",
        load_kernel,
        [observed, mask_bits, frame_factors, pixel_factors],
        [
            struct((rows, width)),
            struct(mask_bits.shape, mask_bits.dtype),
            struct((width, rank)),
            frames_t,
            chunk_t,
            frames_t,
        ],
        in_specs=[HBM] * 4,
        scratch=[DMA((7,))],
    )
    def step(visit, chunk, block, frames, done, wanted):
        at = chunk * size
        first = done is None
        whole = block.shape[0] > size
        columns = visit * width + at

        def kernel(wanted, bits, block, frames, *refs):
            block = block[at : at + size] if whole else block[...]
            new, grad = tile(
                frames[...], block, wanted[:, columns : columns + size], flags(bits, visit * width + at, size)
            )
            refs[-2][...] = new
            refs[-1][...] = added(frames[...], None if first else refs[0][...], grad)

        args = [wanted, bits, block, frames] + ([] if first else [done])
        return call(
            "step",
            kernel,
            args,
            [chunk_t, frames_t],
            aliases={} if first else {4: 1},
            flops=LAST_FLOPS if visit == visits - 1 else 0,
        )

    later, new = lax.optimization_barrier((whole, new))
    coming = [shifted(new, "blk")]
    for c in range(1, CHUNKS):
        new, done = step(0, c, pixels, frames, done, observed0)
        coming.append(shifted(new, "blk"))

    for visit in range(1, visits - 1):
        axis = "blk" if visit < visits - 2 else "wide"
        frames, done = done, None
        sent = []
        for c in range(CHUNKS):
            new, done = step(visit, c, coming[c], frames, done, later)
            sent.append(shifted(new, axis))
        coming = sent

    frames, done = done, None
    visit = visits - 1
    made = []
    for c in range(CHUNKS - 1):
        new, done = step(visit, c, coming[c], frames, done, later)
        made.append(new)

    def last_kernel(wanted, bits, block, frames, done, *refs):
        made, (frames_out, pixels_out, new, sum_v, sems) = refs[: CHUNKS - 1], refs[CHUNKS - 1 :]
        copies = [
            pltpu.make_async_copy(ref, pixels_out.at[c * size : (c + 1) * size], sems.at[c])
            for c, ref in enumerate(made)
        ]
        at = width - size
        copies.append(pltpu.make_async_copy(new, pixels_out.at[at:], sems.at[CHUNKS - 1]))
        copies.append(pltpu.make_async_copy(sum_v, frames_out, sems.at[CHUNKS]))
        for copy in copies[: CHUNKS - 1]:
            copy.start()
        columns = visit * width + at
        new[...], grad = tile(
            frames[...], block[...], wanted[:, columns : columns + size], flags(bits, visit * width + at, size)
        )
        copies[-2].start()
        sum_v[...] = added(frames[...], done[...], grad)
        copies[-1].start()
        for copy in copies:
            copy.wait()

    return call(
        "last",
        last_kernel,
        [later, bits, coming[-1], frames, done, *made],
        [frames_t, struct((width, rank))],
        out_specs=[HBM] * 2,
        scratch=[pltpu.VMEM((size, rank), LOW), pltpu.VMEM((rows, rank), jnp.float32), DMA((CHUNKS + 1,))],
        flops=LAST_FLOPS,
    )


def solution(mesh):
    spec = P(("blk", "wide"), None)
    return jax.shard_map(
        body, mesh=mesh, in_specs=(spec,) * 4, out_specs=(spec, spec), check_vma=False
    )
```

```python
import jax
import jax.numpy as jnp
from jax import lax
from jax.experimental import pallas as pl
from jax.experimental.pallas import tpu as pltpu
from jax.sharding import PartitionSpec as P

CHUNKS = 4
LAST_FLOPS = 200_000_000

step_frames = 0.01
step_pixels = 0.02
decay_weight = 0.1

LOW = jnp.bfloat16
VMEM = pl.BlockSpec(memory_space=pltpu.VMEM)
HBM = pl.BlockSpec(memory_space=pltpu.HBM)
DMA = pltpu.SemaphoreType.DMA


def shifted(value, axis):
    count = lax.axis_size(axis)
    return lax.ppermute(value, axis, [(s, (s + 1) % count) for s in range(count)])


def swapped(value):
    count = lax.axis_size("blk")
    return lax.ppermute(value, "blk", [(s, s + 1 - 2 * (s % 2)) for s in range(count)])


def is_odd():
    return lax.axis_index("blk") % 2 == 1


def struct(shape, dtype=LOW):
    return jax.ShapeDtypeStruct(shape, dtype)


def call(name, kernel, args, outs, in_specs=None, out_specs=None, scratch=(), aliases=None, flops=0):
    return pl.pallas_call(
        kernel,
        name=name,
        out_shape=tuple(outs),
        in_specs=in_specs or [VMEM] * len(args),
        out_specs=tuple(out_specs or [VMEM] * len(outs)),
        scratch_shapes=list(scratch),
        input_output_aliases=aliases or {},
        compiler_params=pltpu.CompilerParams(vmem_limit_bytes=24 * 1024 * 1024),
        cost_estimate=pl.CostEstimate(flops=flops, bytes_accessed=0, transcendentals=0),
    )(*args)


def flags(bits, lower, count):
    words = bits.shape[1]
    pieces = []
    at = lower
    while at < lower + count:
        flag, word = divmod(at, words)
        size = min(words - word, lower + count - at)
        pieces.append(lax.shift_right_logical(bits[:, word : word + size], flag) & 1)
        at += size
    return pieces[0] if len(pieces) == 1 else jnp.concatenate(pieces, axis=1)


def tile(frames, block, wanted, visible):
    frames_low = frames.astype(LOW)
    predicted = lax.dot_general(
        frames_low, block, (((1,), (1,)), ((), ())), preferred_element_type=jnp.float32
    )
    errors = wanted.astype(jnp.float32) - predicted
    clipped = jnp.clip(errors, -1.0, 1.0)
    scaled = jnp.where(visible != 0, clipped, 0.0).astype(LOW)
    grad_pixels = lax.dot_general(
        scaled, frames_low, (((0,), (0,)), ((), ())), preferred_element_type=jnp.float32
    )
    current = block.astype(jnp.float32)
    new = (current + step_pixels * (grad_pixels - decay_weight * current)).astype(LOW)
    return new, jnp.dot(scaled, block, preferred_element_type=jnp.float32)


def added(frames, done, grad):
    if done is None:
        return frames + step_frames * (grad - decay_weight * frames)
    return done + step_frames * grad


def body(observed, mask_bits, frame_factors, pixel_factors):
    width, rank = pixel_factors.shape
    rows = frame_factors.shape[0]
    visits = observed.shape[1] // width
    size = width // CHUNKS
    chunk_t = struct((size, rank))
    frames_t = struct((rows, rank), jnp.float32)
    early = 2 * size
    early_words = min(early, mask_bits.shape[1])

    def load_kernel(observed, mask_bits, frames_in, pixels_in, new, done, wanted, bits, frames, pixels, sems):
        @pl.when(is_odd())
        def _():
            copies = [
                pltpu.make_async_copy(mask_bits.at[:, :early_words], bits, sems.at[0]),
                pltpu.make_async_copy(pixels_in.at[:early], pixels, sems.at[1]),
                pltpu.make_async_copy(observed.at[:, :early], wanted, sems.at[2]),
                pltpu.make_async_copy(frames_in, frames, sems.at[3]),
            ]
            for copy in copies:
                copy.start()
            for copy in copies:
                copy.wait()
            new[...], grad = tile(frames[...], pixels[...], wanted[...], flags(bits, 0, early))
            done[...] = added(frames[...], None, grad)

    new, done = call(
        "load",
        load_kernel,
        [
            pltpu.with_memory_space_constraint(a, pltpu.HBM)
            for a in (observed, mask_bits, frame_factors, pixel_factors)
        ],
        [struct((early, rank)), frames_t],
        in_specs=[HBM] * 4,
        scratch=[
            pltpu.VMEM((rows, early), LOW),
            pltpu.VMEM((rows, early_words), mask_bits.dtype),
            pltpu.VMEM((rows, rank), jnp.float32),
            pltpu.VMEM((early, rank), LOW),
            DMA((4,)),
        ],
    )
    later, new = lax.optimization_barrier((observed, new))
    arrived = shifted(new, "blk")
    observed0, bits, pixels, frames = observed[:, :width], mask_bits, pixel_factors, frame_factors

    def third_kernel(observed0, bits, pixels, frames, done, new, done_out):
        new[...], grad = tile(
            frames[...],
            pixels[early : early + size],
            observed0[:, early : early + size],
            flags(bits, early, size),
        )
        start = added(frames[...], None, jnp.zeros_like(grad))
        done_out[...] = jnp.where(is_odd(), done[...], start) + step_frames * grad

    new, done = call(
        "third",
        third_kernel,
        [observed0, bits, pixels, frames, done],
        [chunk_t, frames_t],
        aliases={4: 1},
    )
    third = shifted(new, "blk")

    def even_kernel(observed0, bits, pixels, frames, done, new0, new1, done_out):
        @pl.when(is_odd())
        def _():
            done_out[...] = done[...]

        @pl.when(jnp.logical_not(is_odd()))
        def _():
            made, grad = tile(
                frames[...], pixels[:early], observed0[:, :early], flags(bits, 0, early)
            )
            new0[...] = made[:size]
            new1[...] = made[size:]
            done_out[...] = done[...] + step_frames * grad

    new0, new1, done = call(
        "even",
        even_kernel,
        [observed0, bits, pixels, frames, done],
        [chunk_t, chunk_t, frames_t],
        aliases={4: 2},
    )
    coming = [(arrived, swapped(new0), 0), (arrived, swapped(new1), size), third]

    def step(visit, chunk, block, frames, done, wanted):
        at = chunk * size
        first = done is None
        whole = visit == 0
        columns = visit * width + at

        split = isinstance(block, tuple)

        def kernel(wanted, bits, frames, *refs):
            if split:
                start = block[2]
                held = jnp.where(is_odd(), refs[1][...], refs[0][start : start + size])
                refs = refs[2:]
            else:
                held = refs[0][at : at + size] if whole else refs[0][...]
                refs = refs[1:]
            new, grad = tile(
                frames[...], held, wanted[:, columns : columns + size], flags(bits, visit * width + at, size)
            )
            refs[-2][...] = new
            refs[-1][...] = added(frames[...], None if first else refs[0][...], grad)

        blocks = list(block[:2]) if split else [block]
        args = [wanted, bits, frames, *blocks] + ([] if first else [done])
        return call(
            "step",
            kernel,
            args,
            [chunk_t, frames_t],
            aliases={} if first else {len(args) - 1: 1},
            flops=LAST_FLOPS if visit == visits - 1 else 0,
        )

    for c in range(3, CHUNKS):
        new, done = step(0, c, pixels, frames, done, observed0)
        coming.append(shifted(new, "blk"))

    for visit in range(1, visits - 1):
        axis = "blk" if visit < visits - 2 else "wide"
        frames, done = done, None
        sent = []
        for c in range(CHUNKS):
            new, done = step(visit, c, coming[c], frames, done, later)
            sent.append(shifted(new, axis))
        coming = sent

    frames, done = done, None
    visit = visits - 1
    made = []
    for c in range(CHUNKS - 1):
        new, done = step(visit, c, coming[c], frames, done, later)
        made.append(new)

    def last_kernel(wanted, bits, block, frames, done, *refs):
        made, (frames_out, pixels_out, new, sum_v, sems) = refs[: CHUNKS - 1], refs[CHUNKS - 1 :]
        copies = [
            pltpu.make_async_copy(ref, pixels_out.at[c * size : (c + 1) * size], sems.at[c])
            for c, ref in enumerate(made)
        ]
        at = width - size
        copies.append(pltpu.make_async_copy(new, pixels_out.at[at:], sems.at[CHUNKS - 1]))
        copies.append(pltpu.make_async_copy(sum_v, frames_out, sems.at[CHUNKS]))
        for copy in copies[: CHUNKS - 1]:
            copy.start()
        columns = visit * width + at
        new[...], grad = tile(
            frames[...], block[...], wanted[:, columns : columns + size], flags(bits, visit * width + at, size)
        )
        copies[-2].start()
        sum_v[...] = added(frames[...], done[...], grad)
        copies[-1].start()
        for copy in copies:
            copy.wait()

    return call(
        "last",
        last_kernel,
        [later, bits, coming[-1], frames, done, *made],
        [frames_t, struct((width, rank))],
        out_specs=[HBM] * 2,
        scratch=[pltpu.VMEM((size, rank), LOW), pltpu.VMEM((rows, rank), jnp.float32), DMA((CHUNKS + 1,))],
        flops=LAST_FLOPS,
    )


def solution(mesh):
    spec = P(("blk", "wide"), None)
    return jax.shard_map(
        body, mesh=mesh, in_specs=(spec,) * 4, out_specs=(spec, spec), check_vma=False
    )
```

```python
import jax
import jax.numpy as jnp
from jax import lax
from jax.experimental import pallas as pl
from jax.experimental.pallas import tpu as pltpu
from jax.sharding import PartitionSpec as P

CHUNKS = 4
LAST_FLOPS = 200_000_000

step_frames = 0.01
step_pixels = 0.02
decay_weight = 0.1

LOW = jnp.bfloat16
VMEM = pl.BlockSpec(memory_space=pltpu.VMEM)
HBM = pl.BlockSpec(memory_space=pltpu.HBM)
DMA = pltpu.SemaphoreType.DMA


def shifted(value, axis):
    count = lax.axis_size(axis)
    return lax.ppermute(value, axis, [(s, (s + 1) % count) for s in range(count)])


def swapped(value):
    count = lax.axis_size("blk")
    return lax.ppermute(value, "blk", [(s, s + 1 - 2 * (s % 2)) for s in range(count)])


def is_odd():
    return lax.axis_index("blk") % 2 == 1


def struct(shape, dtype=LOW):
    return jax.ShapeDtypeStruct(shape, dtype)


def call(name, kernel, args, outs, in_specs=None, out_specs=None, scratch=(), aliases=None, flops=0):
    return pl.pallas_call(
        kernel,
        name=name,
        out_shape=tuple(outs),
        in_specs=in_specs or [VMEM] * len(args),
        out_specs=tuple(out_specs or [VMEM] * len(outs)),
        scratch_shapes=list(scratch),
        input_output_aliases=aliases or {},
        compiler_params=pltpu.CompilerParams(vmem_limit_bytes=24 * 1024 * 1024),
        cost_estimate=pl.CostEstimate(flops=flops, bytes_accessed=0, transcendentals=0),
    )(*args)


def flags(bits, lower, count):
    words = bits.shape[1]
    pieces = []
    at = lower
    while at < lower + count:
        flag, word = divmod(at, words)
        size = min(words - word, lower + count - at)
        pieces.append(lax.shift_right_logical(bits[:, word : word + size], flag) & 1)
        at += size
    return pieces[0] if len(pieces) == 1 else jnp.concatenate(pieces, axis=1)


def tile(frames, block, wanted, visible):
    frames_low = frames.astype(LOW)
    predicted = lax.dot_general(
        frames_low, block, (((1,), (1,)), ((), ())), preferred_element_type=jnp.float32
    )
    errors = wanted.astype(jnp.float32) - predicted
    clipped = jnp.clip(errors, -1.0, 1.0)
    scaled = jnp.where(visible != 0, clipped, 0.0).astype(LOW)
    grad_pixels = lax.dot_general(
        scaled, frames_low, (((0,), (0,)), ((), ())), preferred_element_type=jnp.float32
    )
    current = block.astype(jnp.float32)
    new = (current + step_pixels * (grad_pixels - decay_weight * current)).astype(LOW)
    return new, jnp.dot(scaled, block, preferred_element_type=jnp.float32)


def added(frames, done, grad):
    if done is None:
        return frames + step_frames * (grad - decay_weight * frames)
    return done + step_frames * grad


def body(observed, mask_bits, frame_factors, pixel_factors):
    width, rank = pixel_factors.shape
    rows = frame_factors.shape[0]
    visits = observed.shape[1] // width
    size = width // CHUNKS
    chunk_t = struct((size, rank))
    frames_t = struct((rows, rank), jnp.float32)
    early = 2 * size
    early_words = min(early, mask_bits.shape[1])

    def load_kernel(observed, mask_bits, frames_in, pixels_in, new, done, wanted, bits, frames, pixels, sems):
        @pl.when(is_odd())
        def _():
            copies = [
                pltpu.make_async_copy(mask_bits.at[:, :early_words], bits, sems.at[0]),
                pltpu.make_async_copy(pixels_in.at[:early], pixels, sems.at[1]),
                pltpu.make_async_copy(observed.at[:, :early], wanted, sems.at[2]),
                pltpu.make_async_copy(frames_in, frames, sems.at[3]),
            ]
            for copy in copies:
                copy.start()
            for copy in copies:
                copy.wait()
            new[...], grad = tile(frames[...], pixels[...], wanted[...], flags(bits, 0, early))
            done[...] = added(frames[...], None, grad)

    new, done = call(
        "load",
        load_kernel,
        [
            pltpu.with_memory_space_constraint(a, pltpu.HBM)
            for a in (observed, mask_bits, frame_factors, pixel_factors)
        ],
        [struct((early, rank)), frames_t],
        in_specs=[HBM] * 4,
        scratch=[
            pltpu.VMEM((rows, early), LOW),
            pltpu.VMEM((rows, early_words), mask_bits.dtype),
            pltpu.VMEM((rows, rank), jnp.float32),
            pltpu.VMEM((early, rank), LOW),
            DMA((4,)),
        ],
    )
    later, new = lax.optimization_barrier((observed, new))
    arrived = shifted(new, "blk")
    observed0, bits, pixels, frames = observed[:, :width], mask_bits, pixel_factors, frame_factors

    def middle_kernel(observed0, bits, pixels, frames, done, new0, new1, new, done_out):
        end = early + size

        @pl.when(is_odd())
        def _():
            new[...], grad = tile(
                frames[...], pixels[early:end], observed0[:, early:end], flags(bits, early, size)
            )
            done_out[...] = added(frames[...], done[...], grad)

        @pl.when(jnp.logical_not(is_odd()))
        def _():
            made, grad = tile(frames[...], pixels[:end], observed0[:, :end], flags(bits, 0, end))
            new0[...] = made[:size]
            new1[...] = made[size:early]
            new[...] = made[early:]
            done_out[...] = added(frames[...], None, grad)

    new0, new1, new, done = call(
        "middle",
        middle_kernel,
        [observed0, bits, pixels, frames, done],
        [chunk_t, chunk_t, chunk_t, frames_t],
        aliases={4: 3},
    )
    third = shifted(new, "blk")
    coming = [(arrived, swapped(new0), 0), (arrived, swapped(new1), size), third]

    def step(visit, chunk, block, frames, done, wanted):
        at = chunk * size
        first = done is None
        whole = visit == 0
        columns = visit * width + at

        split = isinstance(block, tuple)

        def kernel(wanted, bits, frames, *refs):
            if split:
                start = block[2]
                held = jnp.where(is_odd(), refs[1][...], refs[0][start : start + size])
                refs = refs[2:]
            else:
                held = refs[0][at : at + size] if whole else refs[0][...]
                refs = refs[1:]
            new, grad = tile(
                frames[...], held, wanted[:, columns : columns + size], flags(bits, visit * width + at, size)
            )
            refs[-2][...] = new
            refs[-1][...] = added(frames[...], None if first else refs[0][...], grad)

        blocks = list(block[:2]) if split else [block]
        args = [wanted, bits, frames, *blocks] + ([] if first else [done])
        return call(
            "step",
            kernel,
            args,
            [chunk_t, frames_t],
            aliases={} if first else {len(args) - 1: 1},
            flops=LAST_FLOPS if visit == visits - 1 else 0,
        )

    for c in range(3, CHUNKS):
        new, done = step(0, c, pixels, frames, done, observed0)
        coming.append(shifted(new, "blk"))

    def odd_kernel(wanted, bits, frames, block, new, done):
        @pl.when(is_odd())
        def _():
            new[...], grad = tile(
                frames[...], block[...], wanted[:, width : width + size], flags(bits, width, size)
            )
            done[...] = added(frames[...], None, grad)

    def both_kernel(wanted, bits, frames, block, own, done, new0, new, done_out):
        @pl.when(is_odd())
        def _():
            at = width + size
            new[...], grad = tile(
                frames[...], own[...], wanted[:, at : at + size], flags(bits, at, size)
            )
            done_out[...] = added(frames[...], done[...], grad)

        @pl.when(jnp.logical_not(is_odd()))
        def _():
            made, grad = tile(
                frames[...], block[...], wanted[:, width : width + early], flags(bits, width, early)
            )
            new0[...] = made[:size]
            new[...] = made[size:]
            done_out[...] = added(frames[...], None, grad)

    frames = done
    new, done = call(
        "odd", odd_kernel, [later, bits, frames, coming[0][1]], [chunk_t, frames_t]
    )
    passed = shifted(new, "blk")
    new0, new, done = call(
        "both",
        both_kernel,
        [later, bits, frames, arrived, coming[1][1], done],
        [chunk_t, chunk_t, frames_t],
        aliases={5: 2},
    )
    sent = [(passed, swapped(new0), 0), shifted(new, "blk")]
    for c in range(2, CHUNKS):
        new, done = step(1, c, coming[c], frames, done, later)
        sent.append(shifted(new, "blk"))
    coming = sent

    for visit in range(2, visits - 1):
        axis = "blk" if visit < visits - 2 else "wide"
        frames, done = done, None
        sent = []
        for c in range(CHUNKS):
            new, done = step(visit, c, coming[c], frames, done, later)
            sent.append(shifted(new, axis))
        coming = sent

    frames, done = done, None
    visit = visits - 1
    made = []
    for c in range(CHUNKS - 1):
        new, done = step(visit, c, coming[c], frames, done, later)
        made.append(new)

    def last_kernel(wanted, bits, block, frames, done, *refs):
        made, (frames_out, pixels_out, new, sum_v, sems) = refs[: CHUNKS - 1], refs[CHUNKS - 1 :]
        copies = [
            pltpu.make_async_copy(ref, pixels_out.at[c * size : (c + 1) * size], sems.at[c])
            for c, ref in enumerate(made)
        ]
        at = width - size
        copies.append(pltpu.make_async_copy(new, pixels_out.at[at:], sems.at[CHUNKS - 1]))
        copies.append(pltpu.make_async_copy(sum_v, frames_out, sems.at[CHUNKS]))
        for copy in copies[: CHUNKS - 1]:
            copy.start()
        columns = visit * width + at
        new[...], grad = tile(
            frames[...], block[...], wanted[:, columns : columns + size], flags(bits, visit * width + at, size)
        )
        copies[-2].start()
        sum_v[...] = added(frames[...], done[...], grad)
        copies[-1].start()
        for copy in copies:
            copy.wait()

    return call(
        "last",
        last_kernel,
        [later, bits, coming[-1], frames, done, *made],
        [frames_t, struct((width, rank))],
        out_specs=[HBM] * 2,
        scratch=[pltpu.VMEM((size, rank), LOW), pltpu.VMEM((rows, rank), jnp.float32), DMA((CHUNKS + 1,))],
        flops=LAST_FLOPS,
    )


def solution(mesh):
    spec = P(("blk", "wide"), None)
    return jax.shard_map(
        body, mesh=mesh, in_specs=(spec,) * 4, out_specs=(spec, spec), check_vma=False
    )
```

```python
import jax
import jax.numpy as jnp
from jax import lax
from jax.experimental import pallas as pl
from jax.experimental.pallas import tpu as pltpu
from jax.sharding import PartitionSpec as P

CHUNKS = 4
LAST_FLOPS = 200_000_000

step_frames = 0.01
step_pixels = 0.02
decay_weight = 0.1

LOW = jnp.bfloat16
VMEM = pl.BlockSpec(memory_space=pltpu.VMEM)
HBM = pl.BlockSpec(memory_space=pltpu.HBM)
DMA = pltpu.SemaphoreType.DMA


def shifted(value, axis):
    count = lax.axis_size(axis)
    return lax.ppermute(value, axis, [(s, (s + 1) % count) for s in range(count)])


def swapped(value):
    count = lax.axis_size("blk")
    return lax.ppermute(value, "blk", [(s, s + 1 - 2 * (s % 2)) for s in range(count)])


def is_odd():
    return lax.axis_index("blk") % 2 == 1


def struct(shape, dtype=LOW):
    return jax.ShapeDtypeStruct(shape, dtype)


def call(name, kernel, args, outs, in_specs=None, out_specs=None, scratch=(), aliases=None, flops=0):
    return pl.pallas_call(
        kernel,
        name=name,
        out_shape=tuple(outs),
        in_specs=in_specs or [VMEM] * len(args),
        out_specs=tuple(out_specs or [VMEM] * len(outs)),
        scratch_shapes=list(scratch),
        input_output_aliases=aliases or {},
        compiler_params=pltpu.CompilerParams(vmem_limit_bytes=24 * 1024 * 1024),
        cost_estimate=pl.CostEstimate(flops=flops, bytes_accessed=0, transcendentals=0),
    )(*args)


def flags(bits, lower, count):
    words = bits.shape[1]
    pieces = []
    at = lower
    while at < lower + count:
        flag, word = divmod(at, words)
        size = min(words - word, lower + count - at)
        pieces.append(lax.shift_right_logical(bits[:, word : word + size], flag) & 1)
        at += size
    return pieces[0] if len(pieces) == 1 else jnp.concatenate(pieces, axis=1)


def tile(frames, block, wanted, visible):
    frames_low = frames.astype(LOW)
    scaled = clipped_errors(frames_low, block, wanted, visible)
    return updated(frames_low, block, scaled), jnp.dot(
        scaled, block, preferred_element_type=jnp.float32
    )


def clipped_errors(frames_low, block, wanted, visible):
    predicted = lax.dot_general(
        frames_low, block, (((1,), (1,)), ((), ())), preferred_element_type=jnp.float32
    )
    errors = wanted.astype(jnp.float32) - predicted
    clipped = jnp.clip(errors, -1.0, 1.0)
    return jnp.where(visible != 0, clipped, 0.0).astype(LOW)


def updated(frames_low, block, scaled):
    grad_pixels = lax.dot_general(
        scaled, frames_low, (((0,), (0,)), ((), ())), preferred_element_type=jnp.float32
    )
    current = block.astype(jnp.float32)
    return (current + step_pixels * (grad_pixels - decay_weight * current)).astype(LOW)


def added(frames, done, grad):
    if done is None:
        return frames + step_frames * (grad - decay_weight * frames)
    return done + step_frames * grad


def body(observed, mask_bits, frame_factors, pixel_factors):
    width, rank = pixel_factors.shape
    rows = frame_factors.shape[0]
    visits = observed.shape[1] // width
    size = width // CHUNKS
    chunk_t = struct((size, rank))
    frames_t = struct((rows, rank), jnp.float32)
    early = 2 * size
    early_words = min(early, mask_bits.shape[1])

    def load_kernel(observed, mask_bits, frames_in, pixels_in, new, scaled, wanted, bits, frames, pixels, sems):
        @pl.when(is_odd())
        def _():
            copies = [
                pltpu.make_async_copy(mask_bits.at[:, :early_words], bits, sems.at[0]),
                pltpu.make_async_copy(pixels_in.at[:early], pixels, sems.at[1]),
                pltpu.make_async_copy(observed.at[:, :early], wanted, sems.at[2]),
                pltpu.make_async_copy(frames_in, frames, sems.at[3]),
            ]
            for copy in copies:
                copy.start()
            for copy in copies:
                copy.wait()
            frames_low = frames[...].astype(LOW)
            scaled[...] = clipped_errors(frames_low, pixels[...], wanted[...], flags(bits, 0, early))
            new[...] = updated(frames_low, pixels[...], scaled[...])

    new, scaled = call(
        "load",
        load_kernel,
        [
            pltpu.with_memory_space_constraint(a, pltpu.HBM)
            for a in (observed, mask_bits, frame_factors, pixel_factors)
        ],
        [struct((early, rank)), struct((rows, early))],
        in_specs=[HBM] * 4,
        scratch=[
            pltpu.VMEM((rows, early), LOW),
            pltpu.VMEM((rows, early_words), mask_bits.dtype),
            pltpu.VMEM((rows, rank), jnp.float32),
            pltpu.VMEM((early, rank), LOW),
            DMA((4,)),
        ],
    )
    later, new = lax.optimization_barrier((observed, new))
    arrived = shifted(new, "blk")
    observed0, bits, pixels, frames = observed[:, :width], mask_bits, pixel_factors, frame_factors

    def middle_kernel(observed0, bits, pixels, frames, scaled, new0, new1, new, done):
        end = early + size

        @pl.when(is_odd())
        def _():
            new[...], grad = tile(
                frames[...], pixels[early:end], observed0[:, early:end], flags(bits, early, size)
            )
            early_grad = jnp.dot(scaled[...], pixels[:early], preferred_element_type=jnp.float32)
            done[...] = added(frames[...], None, early_grad + grad)

        @pl.when(jnp.logical_not(is_odd()))
        def _():
            made, grad = tile(frames[...], pixels[:end], observed0[:, :end], flags(bits, 0, end))
            new0[...] = made[:size]
            new1[...] = made[size:early]
            new[...] = made[early:]
            done[...] = added(frames[...], None, grad)

    new0, new1, new, done = call(
        "middle",
        middle_kernel,
        [observed0, bits, pixels, frames, scaled],
        [chunk_t, chunk_t, chunk_t, frames_t],
    )
    third = shifted(new, "blk")
    coming = [(arrived, swapped(new0), 0), (arrived, swapped(new1), size), third]

    def step(visit, chunk, block, frames, done, wanted):
        at = chunk * size
        first = done is None
        whole = visit == 0
        columns = visit * width + at

        split = isinstance(block, tuple)

        def kernel(wanted, bits, frames, *refs):
            if split:
                start = block[2]
                held = jnp.where(is_odd(), refs[1][...], refs[0][start : start + size])
                refs = refs[2:]
            else:
                held = refs[0][at : at + size] if whole else refs[0][...]
                refs = refs[1:]
            new, grad = tile(
                frames[...], held, wanted[:, columns : columns + size], flags(bits, visit * width + at, size)
            )
            refs[-2][...] = new
            refs[-1][...] = added(frames[...], None if first else refs[0][...], grad)

        blocks = list(block[:2]) if split else [block]
        args = [wanted, bits, frames, *blocks] + ([] if first else [done])
        return call(
            "step",
            kernel,
            args,
            [chunk_t, frames_t],
            aliases={} if first else {len(args) - 1: 1},
            flops=LAST_FLOPS if visit == visits - 1 else 0,
        )

    for c in range(3, CHUNKS):
        new, done = step(0, c, pixels, frames, done, observed0)
        coming.append(shifted(new, "blk"))

    def odd_kernel(wanted, bits, frames, block, new, done):
        @pl.when(is_odd())
        def _():
            new[...], grad = tile(
                frames[...], block[...], wanted[:, width : width + size], flags(bits, width, size)
            )
            done[...] = added(frames[...], None, grad)

    def both_kernel(wanted, bits, frames, block, own, done, new0, new, done_out):
        @pl.when(is_odd())
        def _():
            at = width + size
            new[...], grad = tile(
                frames[...], own[...], wanted[:, at : at + size], flags(bits, at, size)
            )
            done_out[...] = added(frames[...], done[...], grad)

        @pl.when(jnp.logical_not(is_odd()))
        def _():
            made, grad = tile(
                frames[...], block[...], wanted[:, width : width + early], flags(bits, width, early)
            )
            new0[...] = made[:size]
            new[...] = made[size:]
            done_out[...] = added(frames[...], None, grad)

    def start_step(visit, block, frames):
        at = visit * width

        def kernel(wanted, bits, frames, block, new, scaled):
            frames_low = frames[...].astype(LOW)
            scaled[...] = clipped_errors(
                frames_low, block[...], wanted[:, at : at + size], flags(bits, at, size)
            )
            new[...] = updated(frames_low, block[...], scaled[...])

        return call(
            "start", kernel, [later, bits, frames, block], [chunk_t, struct((rows, size))]
        )

    def end_step(block, frames, scaled):
        def kernel(block, frames, scaled, done):
            grad = jnp.dot(scaled[...], block[...], preferred_element_type=jnp.float32)
            done[...] = added(frames[...], None, grad)

        return call("end", kernel, [block, frames, scaled], [frames_t])[0]

    frames = done
    new, done = call(
        "odd", odd_kernel, [later, bits, frames, coming[0][1]], [chunk_t, frames_t]
    )
    passed = shifted(new, "blk")
    new0, new, done = call(
        "both",
        both_kernel,
        [later, bits, frames, arrived, coming[1][1], done],
        [chunk_t, chunk_t, frames_t],
        aliases={5: 2},
    )
    sent = [(passed, swapped(new0), 0), shifted(new, "blk")]
    for c in range(2, CHUNKS):
        new, done = step(1, c, coming[c], frames, done, later)
        sent.append(shifted(new, "blk"))
    coming = sent

    for visit in range(2, visits - 1):
        axis = "blk" if visit < visits - 2 else "wide"
        frames, done = done, None
        sent = []
        for c in range(CHUNKS):
            if c == 0 and visit == visits - 2:
                new, scaled = start_step(visit, coming[c], frames)
                sent.append(shifted(new, axis))
                done = end_step(coming[c], frames, scaled)
                continue
            new, done = step(visit, c, coming[c], frames, done, later)
            sent.append(shifted(new, axis))
        coming = sent

    frames, done = done, None
    visit = visits - 1
    made = []
    for c in range(CHUNKS - 1):
        new, done = step(visit, c, coming[c], frames, done, later)
        made.append(new)

    def last_kernel(wanted, bits, block, frames, done, *refs):
        made, (frames_out, pixels_out, new, sum_v, sems) = refs[: CHUNKS - 1], refs[CHUNKS - 1 :]
        copies = [
            pltpu.make_async_copy(ref, pixels_out.at[c * size : (c + 1) * size], sems.at[c])
            for c, ref in enumerate(made)
        ]
        at = width - size
        copies.append(pltpu.make_async_copy(new, pixels_out.at[at:], sems.at[CHUNKS - 1]))
        copies.append(pltpu.make_async_copy(sum_v, frames_out, sems.at[CHUNKS]))
        for copy in copies[: CHUNKS - 1]:
            copy.start()
        columns = visit * width + at
        frames_low = frames[...].astype(LOW)
        scaled = clipped_errors(
            frames_low,
            block[...],
            wanted[:, columns : columns + size],
            flags(bits, visit * width + at, size),
        )
        grad = jnp.dot(scaled, block[...], preferred_element_type=jnp.float32)
        sum_v[...] = added(frames[...], done[...], grad)
        copies[-1].start()
        new[...] = updated(frames_low, block[...], scaled)
        copies[-2].start()
        for copy in copies:
            copy.wait()

    return call(
        "last",
        last_kernel,
        [later, bits, coming[-1], frames, done, *made],
        [frames_t, struct((width, rank))],
        out_specs=[HBM] * 2,
        scratch=[pltpu.VMEM((size, rank), LOW), pltpu.VMEM((rows, rank), jnp.float32), DMA((CHUNKS + 1,))],
        flops=LAST_FLOPS,
    )


def solution(mesh):
    spec = P(("blk", "wide"), None)
    return jax.shard_map(
        body, mesh=mesh, in_specs=(spec,) * 4, out_specs=(spec, spec), check_vma=False
    )
```

```python
import jax
import jax.numpy as jnp
from jax import lax
from jax.experimental import pallas as pl
from jax.experimental.pallas import tpu as pltpu
from jax.sharding import PartitionSpec as P

CHUNKS = 4
LAST_FLOPS = 200_000_000

step_frames = 0.01
step_pixels = 0.02
decay_weight = 0.1

LOW = jnp.bfloat16
VMEM = pl.BlockSpec(memory_space=pltpu.VMEM)
HBM = pl.BlockSpec(memory_space=pltpu.HBM)
DMA = pltpu.SemaphoreType.DMA


def shifted(value, axis):
    count = lax.axis_size(axis)
    return lax.ppermute(value, axis, [(s, (s + 1) % count) for s in range(count)])


def swapped(value):
    count = lax.axis_size("blk")
    return lax.ppermute(value, "blk", [(s, s + 1 - 2 * (s % 2)) for s in range(count)])


def is_odd():
    return lax.axis_index("blk") % 2 == 1


def struct(shape, dtype=LOW):
    return jax.ShapeDtypeStruct(shape, dtype)


def call(name, kernel, args, outs, in_specs=None, out_specs=None, scratch=(), aliases=None, flops=0):
    return pl.pallas_call(
        kernel,
        name=name,
        out_shape=tuple(outs),
        in_specs=in_specs or [VMEM] * len(args),
        out_specs=tuple(out_specs or [VMEM] * len(outs)),
        scratch_shapes=list(scratch),
        input_output_aliases=aliases or {},
        compiler_params=pltpu.CompilerParams(vmem_limit_bytes=24 * 1024 * 1024),
        cost_estimate=pl.CostEstimate(flops=flops, bytes_accessed=0, transcendentals=0),
    )(*args)


def flags(bits, lower, count):
    words = bits.shape[1]
    pieces = []
    at = lower
    while at < lower + count:
        flag, word = divmod(at, words)
        size = min(words - word, lower + count - at)
        pieces.append(lax.shift_right_logical(bits[:, word : word + size], flag) & 1)
        at += size
    return pieces[0] if len(pieces) == 1 else jnp.concatenate(pieces, axis=1)


def tile(frames, block, wanted, visible):
    frames_low = frames.astype(LOW)
    scaled = clipped_errors(frames_low, block, wanted, visible)
    return updated(frames_low, block, scaled), jnp.dot(
        scaled, block, preferred_element_type=jnp.float32
    )


def product(frames_low, block):
    return lax.dot_general(
        frames_low, block, (((1,), (1,)), ((), ())), preferred_element_type=jnp.float32
    )


def clipped_errors(frames_low, block, wanted, visible):
    return clipped_rest(product(frames_low, block), wanted, visible)


def clipped_rest(predicted, wanted, visible):
    errors = wanted.astype(jnp.float32) - predicted
    clipped = jnp.clip(errors, -1.0, 1.0)
    return jnp.where(visible != 0, clipped, 0.0).astype(LOW)


def updated(frames_low, block, scaled):
    grad_pixels = lax.dot_general(
        scaled, frames_low, (((0,), (0,)), ((), ())), preferred_element_type=jnp.float32
    )
    current = block.astype(jnp.float32)
    return (current + step_pixels * (grad_pixels - decay_weight * current)).astype(LOW)


def added(frames, done, grad):
    if done is None:
        return frames + step_frames * (grad - decay_weight * frames)
    return done + step_frames * grad


def body(observed, mask_bits, frame_factors, pixel_factors):
    width, rank = pixel_factors.shape
    rows = frame_factors.shape[0]
    visits = observed.shape[1] // width
    size = width // CHUNKS
    chunk_t = struct((size, rank))
    frames_t = struct((rows, rank), jnp.float32)
    early = 2 * size
    early_words = min(early, mask_bits.shape[1])

    def load_kernel(observed, mask_bits, frames_in, pixels_in, new, scaled, wanted, bits, frames, pixels, predicted, sems):
        @pl.when(is_odd())
        def _():
            copies = [
                pltpu.make_async_copy(frames_in, frames, sems.at[0]),
                pltpu.make_async_copy(pixels_in.at[:early], pixels, sems.at[1]),
                pltpu.make_async_copy(mask_bits.at[:, :early_words], bits, sems.at[2]),
                pltpu.make_async_copy(observed.at[:, :early], wanted, sems.at[3]),
            ]
            for copy in copies:
                copy.start()
            for copy in copies[:2]:
                copy.wait()
            frames_low = frames[...].astype(LOW)
            predicted[...] = product(frames_low, pixels[...])
            for copy in copies[2:]:
                copy.wait()
            scaled[...] = clipped_rest(predicted[...], wanted[...], flags(bits, 0, early))
            new[...] = updated(frames_low, pixels[...], scaled[...])

    new, scaled = call(
        "load",
        load_kernel,
        [
            pltpu.with_memory_space_constraint(a, pltpu.HBM)
            for a in (observed, mask_bits, frame_factors, pixel_factors)
        ],
        [struct((early, rank)), struct((rows, early))],
        in_specs=[HBM] * 4,
        scratch=[
            pltpu.VMEM((rows, early), LOW),
            pltpu.VMEM((rows, early_words), mask_bits.dtype),
            pltpu.VMEM((rows, rank), jnp.float32),
            pltpu.VMEM((early, rank), LOW),
            pltpu.VMEM((rows, early), jnp.float32),
            DMA((4,)),
        ],
    )
    later, new = lax.optimization_barrier((observed, new))
    arrived = shifted(new, "blk")
    observed0, bits, pixels, frames = observed[:, :width], mask_bits, pixel_factors, frame_factors

    def middle_kernel(observed0, bits, pixels, frames, scaled, new0, new1, new, done):
        end = early + size

        @pl.when(is_odd())
        def _():
            new[...], grad = tile(
                frames[...], pixels[early:end], observed0[:, early:end], flags(bits, early, size)
            )
            early_grad = jnp.dot(scaled[...], pixels[:early], preferred_element_type=jnp.float32)
            done[...] = added(frames[...], None, early_grad + grad)

        @pl.when(jnp.logical_not(is_odd()))
        def _():
            made, grad = tile(frames[...], pixels[:end], observed0[:, :end], flags(bits, 0, end))
            new0[...] = made[:size]
            new1[...] = made[size:early]
            new[...] = made[early:]
            done[...] = added(frames[...], None, grad)

    new0, new1, new, done = call(
        "middle",
        middle_kernel,
        [observed0, bits, pixels, frames, scaled],
        [chunk_t, chunk_t, chunk_t, frames_t],
    )
    third = shifted(new, "blk")
    coming = [(arrived, swapped(new0), 0), (arrived, swapped(new1), size), third]

    def step(visit, chunk, block, frames, done, wanted):
        at = chunk * size
        first = done is None
        whole = visit == 0
        columns = visit * width + at

        split = isinstance(block, tuple)

        def kernel(wanted, bits, frames, *refs):
            if split:
                start = block[2]
                held = jnp.where(is_odd(), refs[1][...], refs[0][start : start + size])
                refs = refs[2:]
            else:
                held = refs[0][at : at + size] if whole else refs[0][...]
                refs = refs[1:]
            new, grad = tile(
                frames[...], held, wanted[:, columns : columns + size], flags(bits, visit * width + at, size)
            )
            refs[-2][...] = new
            refs[-1][...] = added(frames[...], None if first else refs[0][...], grad)

        blocks = list(block[:2]) if split else [block]
        args = [wanted, bits, frames, *blocks] + ([] if first else [done])
        return call(
            "step",
            kernel,
            args,
            [chunk_t, frames_t],
            aliases={} if first else {len(args) - 1: 1},
            flops=LAST_FLOPS if visit == visits - 1 else 0,
        )

    for c in range(3, CHUNKS):
        new, done = step(0, c, pixels, frames, done, observed0)
        coming.append(shifted(new, "blk"))

    def odd_kernel(wanted, bits, frames, block, new, done):
        @pl.when(is_odd())
        def _():
            new[...], grad = tile(
                frames[...], block[...], wanted[:, width : width + size], flags(bits, width, size)
            )
            done[...] = added(frames[...], None, grad)

    def both_kernel(wanted, bits, frames, block, own, done, new0, new, done_out):
        @pl.when(is_odd())
        def _():
            at = width + size
            new[...], grad = tile(
                frames[...], own[...], wanted[:, at : at + size], flags(bits, at, size)
            )
            done_out[...] = added(frames[...], done[...], grad)

        @pl.when(jnp.logical_not(is_odd()))
        def _():
            made, grad = tile(
                frames[...], block[...], wanted[:, width : width + early], flags(bits, width, early)
            )
            new0[...] = made[:size]
            new[...] = made[size:]
            done_out[...] = added(frames[...], None, grad)

    def start_step(visit, block, frames):
        at = visit * width

        def kernel(wanted, bits, frames, block, new, scaled):
            frames_low = frames[...].astype(LOW)
            scaled[...] = clipped_errors(
                frames_low, block[...], wanted[:, at : at + size], flags(bits, at, size)
            )
            new[...] = updated(frames_low, block[...], scaled[...])

        return call(
            "start", kernel, [later, bits, frames, block], [chunk_t, struct((rows, size))]
        )

    def end_step(block, frames, scaled):
        def kernel(block, frames, scaled, done):
            grad = jnp.dot(scaled[...], block[...], preferred_element_type=jnp.float32)
            done[...] = added(frames[...], None, grad)

        return call("end", kernel, [block, frames, scaled], [frames_t])[0]

    frames = done
    new, done = call(
        "odd", odd_kernel, [later, bits, frames, coming[0][1]], [chunk_t, frames_t]
    )
    passed = shifted(new, "blk")
    new0, new, done = call(
        "both",
        both_kernel,
        [later, bits, frames, arrived, coming[1][1], done],
        [chunk_t, chunk_t, frames_t],
        aliases={5: 2},
    )
    sent = [(passed, swapped(new0), 0), shifted(new, "blk")]
    for c in range(2, CHUNKS):
        new, done = step(1, c, coming[c], frames, done, later)
        sent.append(shifted(new, "blk"))
    coming = sent

    for visit in range(2, visits - 1):
        axis = "blk" if visit < visits - 2 else "wide"
        frames, done = done, None
        sent = []
        for c in range(CHUNKS):
            if c == 0 and visit == visits - 2:
                new, scaled = start_step(visit, coming[c], frames)
                sent.append(shifted(new, axis))
                done = end_step(coming[c], frames, scaled)
                continue
            new, done = step(visit, c, coming[c], frames, done, later)
            sent.append(shifted(new, axis))
        coming = sent

    frames, done = done, None
    visit = visits - 1
    made = []
    for c in range(CHUNKS - 1):
        new, done = step(visit, c, coming[c], frames, done, later)
        made.append(new)

    def last_kernel(wanted, bits, block, frames, done, *refs):
        made, (frames_out, pixels_out, new, sum_v, sems) = refs[: CHUNKS - 1], refs[CHUNKS - 1 :]
        copies = [
            pltpu.make_async_copy(ref, pixels_out.at[c * size : (c + 1) * size], sems.at[c])
            for c, ref in enumerate(made)
        ]
        at = width - size
        copies.append(pltpu.make_async_copy(new, pixels_out.at[at:], sems.at[CHUNKS - 1]))
        copies.append(pltpu.make_async_copy(sum_v, frames_out, sems.at[CHUNKS]))
        for copy in copies[: CHUNKS - 1]:
            copy.start()
        columns = visit * width + at
        frames_low = frames[...].astype(LOW)
        scaled = clipped_errors(
            frames_low,
            block[...],
            wanted[:, columns : columns + size],
            flags(bits, visit * width + at, size),
        )
        grad = jnp.dot(scaled, block[...], preferred_element_type=jnp.float32)
        sum_v[...] = added(frames[...], done[...], grad)
        copies[-1].start()
        new[...] = updated(frames_low, block[...], scaled)
        copies[-2].start()
        for copy in copies:
            copy.wait()

    return call(
        "last",
        last_kernel,
        [later, bits, coming[-1], frames, done, *made],
        [frames_t, struct((width, rank))],
        out_specs=[HBM] * 2,
        scratch=[pltpu.VMEM((size, rank), LOW), pltpu.VMEM((rows, rank), jnp.float32), DMA((CHUNKS + 1,))],
        flops=LAST_FLOPS,
    )


def solution(mesh):
    spec = P(("blk", "wide"), None)
    return jax.shard_map(
        body, mesh=mesh, in_specs=(spec,) * 4, out_specs=(spec, spec), check_vma=False
    )
```

```python
import jax
import jax.numpy as jnp
from jax import lax
from jax.experimental import pallas as pl
from jax.experimental.pallas import tpu as pltpu
from jax.sharding import PartitionSpec as P

CHUNKS = 4
LAST_FLOPS = 200_000_000

step_frames = 0.01
step_pixels = 0.02
decay_weight = 0.1

LOW = jnp.bfloat16
VMEM = pl.BlockSpec(memory_space=pltpu.VMEM)
HBM = pl.BlockSpec(memory_space=pltpu.HBM)
DMA = pltpu.SemaphoreType.DMA


def shifted(value, axis):
    count = lax.axis_size(axis)
    return lax.ppermute(value, axis, [(s, (s + 1) % count) for s in range(count)])


def swapped(value):
    count = lax.axis_size("blk")
    return lax.ppermute(value, "blk", [(s, s + 1 - 2 * (s % 2)) for s in range(count)])


def is_odd():
    return lax.axis_index("blk") % 2 == 1


def struct(shape, dtype=LOW):
    return jax.ShapeDtypeStruct(shape, dtype)


def call(name, kernel, args, outs, in_specs=None, out_specs=None, scratch=(), aliases=None, flops=0):
    return pl.pallas_call(
        kernel,
        name=name,
        out_shape=tuple(outs),
        in_specs=in_specs or [VMEM] * len(args),
        out_specs=tuple(out_specs or [VMEM] * len(outs)),
        scratch_shapes=list(scratch),
        input_output_aliases=aliases or {},
        compiler_params=pltpu.CompilerParams(vmem_limit_bytes=24 * 1024 * 1024),
        cost_estimate=pl.CostEstimate(flops=flops, bytes_accessed=0, transcendentals=0),
    )(*args)


def flags(bits, lower, count):
    words = bits.shape[1]
    pieces = []
    at = lower
    while at < lower + count:
        flag, word = divmod(at, words)
        size = min(words - word, lower + count - at)
        pieces.append(lax.shift_right_logical(bits[:, word : word + size], flag) & 1)
        at += size
    return pieces[0] if len(pieces) == 1 else jnp.concatenate(pieces, axis=1)


def tile(frames, block, wanted, visible):
    frames_low = frames.astype(LOW)
    scaled = clipped_errors(frames_low, block, wanted, visible)
    return updated(frames_low, block, scaled), jnp.dot(
        scaled, block, preferred_element_type=jnp.float32
    )


def product(frames_low, block):
    return lax.dot_general(
        frames_low, block, (((1,), (1,)), ((), ())), preferred_element_type=jnp.float32
    )


def clipped_errors(frames_low, block, wanted, visible):
    return clipped_rest(product(frames_low, block), wanted, visible)


def clipped_rest(predicted, wanted, visible):
    errors = wanted.astype(jnp.float32) - predicted
    clipped = jnp.clip(errors, -1.0, 1.0)
    return jnp.where(visible != 0, clipped, 0.0).astype(LOW)


def updated(frames_low, block, scaled):
    grad_pixels = lax.dot_general(
        scaled, frames_low, (((0,), (0,)), ((), ())), preferred_element_type=jnp.float32
    )
    current = block.astype(jnp.float32)
    return (current + step_pixels * (grad_pixels - decay_weight * current)).astype(LOW)


def added(frames, done, grad):
    if done is None:
        return frames + step_frames * (grad - decay_weight * frames)
    return done + step_frames * grad


def body(observed, mask_bits, frame_factors, pixel_factors):
    width, rank = pixel_factors.shape
    rows = frame_factors.shape[0]
    visits = observed.shape[1] // width
    size = width // CHUNKS
    chunk_t = struct((size, rank))
    frames_t = struct((rows, rank), jnp.float32)
    early = 2 * size
    early_words = min(early, mask_bits.shape[1])

    def load_kernel(observed, mask_bits, frames_in, pixels_in, new, scaled, wanted, bits, frames, pixels, predicted, sems):
        @pl.when(is_odd())
        def _():
            copies = [
                pltpu.make_async_copy(frames_in, frames, sems.at[0]),
                pltpu.make_async_copy(pixels_in.at[:early], pixels, sems.at[1]),
                pltpu.make_async_copy(mask_bits.at[:, :early_words], bits, sems.at[2]),
                pltpu.make_async_copy(observed.at[:, :early], wanted, sems.at[3]),
            ]
            for copy in copies:
                copy.start(priority=1)
            for copy in copies[:2]:
                copy.wait()
            frames_low = frames[...].astype(LOW)
            predicted[...] = product(frames_low, pixels[...])
            for copy in copies[2:]:
                copy.wait()
            scaled[...] = clipped_rest(predicted[...], wanted[...], flags(bits, 0, early))
            new[...] = updated(frames_low, pixels[...], scaled[...])

    new, scaled = call(
        "load",
        load_kernel,
        [
            pltpu.with_memory_space_constraint(a, pltpu.HBM)
            for a in (observed, mask_bits, frame_factors, pixel_factors)
        ],
        [struct((early, rank)), struct((rows, early))],
        in_specs=[HBM] * 4,
        scratch=[
            pltpu.VMEM((rows, early), LOW),
            pltpu.VMEM((rows, early_words), mask_bits.dtype),
            pltpu.VMEM((rows, rank), jnp.float32),
            pltpu.VMEM((early, rank), LOW),
            pltpu.VMEM((rows, early), jnp.float32),
            DMA((4,)),
        ],
    )
    later, new = lax.optimization_barrier((observed, new))
    arrived = shifted(new, "blk")
    observed0, bits, pixels, frames = observed[:, :width], mask_bits, pixel_factors, frame_factors

    def middle_kernel(observed0, bits, pixels, frames, scaled, new0, new1, new, done):
        end = early + size

        @pl.when(is_odd())
        def _():
            new[...], grad = tile(
                frames[...], pixels[early:end], observed0[:, early:end], flags(bits, early, size)
            )
            early_grad = jnp.dot(scaled[...], pixels[:early], preferred_element_type=jnp.float32)
            done[...] = added(frames[...], None, early_grad + grad)

        @pl.when(jnp.logical_not(is_odd()))
        def _():
            made, grad = tile(frames[...], pixels[:end], observed0[:, :end], flags(bits, 0, end))
            new0[...] = made[:size]
            new1[...] = made[size:early]
            new[...] = made[early:]
            done[...] = added(frames[...], None, grad)

    new0, new1, new, done = call(
        "middle",
        middle_kernel,
        [observed0, bits, pixels, frames, scaled],
        [chunk_t, chunk_t, chunk_t, frames_t],
    )
    third = shifted(new, "blk")
    coming = [(arrived, swapped(new0), 0), (arrived, swapped(new1), size), third]

    def step(visit, chunk, block, frames, done, wanted):
        at = chunk * size
        first = done is None
        whole = visit == 0
        columns = visit * width + at

        split = isinstance(block, tuple)

        def kernel(wanted, bits, frames, *refs):
            if split:
                start = block[2]
                held = jnp.where(is_odd(), refs[1][...], refs[0][start : start + size])
                refs = refs[2:]
            else:
                held = refs[0][at : at + size] if whole else refs[0][...]
                refs = refs[1:]
            new, grad = tile(
                frames[...], held, wanted[:, columns : columns + size], flags(bits, visit * width + at, size)
            )
            refs[-2][...] = new
            refs[-1][...] = added(frames[...], None if first else refs[0][...], grad)

        blocks = list(block[:2]) if split else [block]
        args = [wanted, bits, frames, *blocks] + ([] if first else [done])
        return call(
            "step",
            kernel,
            args,
            [chunk_t, frames_t],
            aliases={} if first else {len(args) - 1: 1},
            flops=LAST_FLOPS if visit == visits - 1 else 0,
        )

    for c in range(3, CHUNKS):
        new, done = step(0, c, pixels, frames, done, observed0)
        coming.append(shifted(new, "blk"))

    def odd_kernel(wanted, bits, frames, block, new, done):
        @pl.when(is_odd())
        def _():
            new[...], grad = tile(
                frames[...], block[...], wanted[:, width : width + size], flags(bits, width, size)
            )
            done[...] = added(frames[...], None, grad)

    def both_kernel(wanted, bits, frames, block, own, done, new0, new, done_out):
        @pl.when(is_odd())
        def _():
            at = width + size
            new[...], grad = tile(
                frames[...], own[...], wanted[:, at : at + size], flags(bits, at, size)
            )
            done_out[...] = added(frames[...], done[...], grad)

        @pl.when(jnp.logical_not(is_odd()))
        def _():
            made, grad = tile(
                frames[...], block[...], wanted[:, width : width + early], flags(bits, width, early)
            )
            new0[...] = made[:size]
            new[...] = made[size:]
            done_out[...] = added(frames[...], None, grad)

    def start_step(visit, block, frames):
        at = visit * width

        def kernel(wanted, bits, frames, block, new, scaled):
            frames_low = frames[...].astype(LOW)
            scaled[...] = clipped_errors(
                frames_low, block[...], wanted[:, at : at + size], flags(bits, at, size)
            )
            new[...] = updated(frames_low, block[...], scaled[...])

        return call(
            "start", kernel, [later, bits, frames, block], [chunk_t, struct((rows, size))]
        )

    def end_step(block, frames, scaled):
        def kernel(block, frames, scaled, done):
            grad = jnp.dot(scaled[...], block[...], preferred_element_type=jnp.float32)
            done[...] = added(frames[...], None, grad)

        return call("end", kernel, [block, frames, scaled], [frames_t])[0]

    frames = done
    new, done = call(
        "odd", odd_kernel, [later, bits, frames, coming[0][1]], [chunk_t, frames_t]
    )
    passed = shifted(new, "blk")
    new0, new, done = call(
        "both",
        both_kernel,
        [later, bits, frames, arrived, coming[1][1], done],
        [chunk_t, chunk_t, frames_t],
        aliases={5: 2},
    )
    sent = [(passed, swapped(new0), 0), shifted(new, "blk")]
    for c in range(2, CHUNKS):
        new, done = step(1, c, coming[c], frames, done, later)
        sent.append(shifted(new, "blk"))
    coming = sent

    for visit in range(2, visits - 1):
        axis = "blk" if visit < visits - 2 else "wide"
        frames, done = done, None
        sent = []
        for c in range(CHUNKS):
            if c == 0 and visit == visits - 2:
                new, scaled = start_step(visit, coming[c], frames)
                sent.append(shifted(new, axis))
                done = end_step(coming[c], frames, scaled)
                continue
            new, done = step(visit, c, coming[c], frames, done, later)
            sent.append(shifted(new, axis))
        coming = sent

    frames, done = done, None
    visit = visits - 1
    written = None
    for c in range(CHUNKS - 1):
        new, done = step(visit, c, coming[c], frames, done, later)

        def write_kernel(new, *refs, at=c * size):
            pixels_out, sem = refs[-2:]
            copy = pltpu.make_async_copy(new, pixels_out.at[at : at + size], sem)
            copy.start()
            copy.wait()

        first = written is None
        written = call(
            "write",
            write_kernel,
            [new] if first else [new, written],
            [struct((width, rank))],
            in_specs=[VMEM] if first else [VMEM, HBM],
            out_specs=[HBM],
            scratch=[DMA],
            aliases={} if first else {1: 0},
            flops=LAST_FLOPS,
        )[0]

    def last_kernel(wanted, bits, block, frames, done, written, frames_out, pixels_out, new, sum_v, sems):
        del written
        at = width - size
        copies = [
            pltpu.make_async_copy(new, pixels_out.at[at:], sems.at[0]),
            pltpu.make_async_copy(sum_v, frames_out, sems.at[1]),
        ]
        columns = visit * width + at
        frames_low = frames[...].astype(LOW)
        scaled = clipped_errors(
            frames_low,
            block[...],
            wanted[:, columns : columns + size],
            flags(bits, visit * width + at, size),
        )
        grad = jnp.dot(scaled, block[...], preferred_element_type=jnp.float32)
        sum_v[...] = added(frames[...], done[...], grad)
        copies[-1].start(priority=1)
        new[...] = updated(frames_low, block[...], scaled)
        copies[0].start()
        for copy in copies:
            copy.wait()

    return call(
        "last",
        last_kernel,
        [later, bits, coming[-1], frames, done, written],
        [frames_t, struct((width, rank))],
        in_specs=[VMEM] * 5 + [HBM],
        out_specs=[HBM] * 2,
        aliases={5: 1},
        scratch=[pltpu.VMEM((size, rank), LOW), pltpu.VMEM((rows, rank), jnp.float32), DMA((2,))],
        flops=LAST_FLOPS,
    )


def solution(mesh):
    spec = P(("blk", "wide"), None)
    return jax.shard_map(
        body, mesh=mesh, in_specs=(spec,) * 4, out_specs=(spec, spec), check_vma=False
    )
```

```python
import jax
import jax.numpy as jnp
from jax import lax
from jax.experimental import pallas as pl
from jax.experimental.pallas import tpu as pltpu
from jax.sharding import PartitionSpec as P

CHUNKS = 4
LAST_FLOPS = 200_000_000

step_frames = 0.01
step_pixels = 0.02
decay_weight = 0.1

LOW = jnp.bfloat16
VMEM = pl.BlockSpec(memory_space=pltpu.VMEM)
HBM = pl.BlockSpec(memory_space=pltpu.HBM)
DMA = pltpu.SemaphoreType.DMA


def shifted(value, axis):
    count = lax.axis_size(axis)
    return lax.ppermute(value, axis, [(s, (s + 1) % count) for s in range(count)])


def swapped(value):
    count = lax.axis_size("blk")
    return lax.ppermute(value, "blk", [(s, s + 1 - 2 * (s % 2)) for s in range(count)])


def is_odd():
    return lax.axis_index("blk") % 2 == 1


def struct(shape, dtype=LOW):
    return jax.ShapeDtypeStruct(shape, dtype)


def call(name, kernel, args, outs, in_specs=None, out_specs=None, scratch=(), aliases=None, flops=0):
    return pl.pallas_call(
        kernel,
        name=name,
        out_shape=tuple(outs),
        in_specs=in_specs or [VMEM] * len(args),
        out_specs=tuple(out_specs or [VMEM] * len(outs)),
        scratch_shapes=list(scratch),
        input_output_aliases=aliases or {},
        compiler_params=pltpu.CompilerParams(vmem_limit_bytes=24 * 1024 * 1024),
        cost_estimate=pl.CostEstimate(flops=flops, bytes_accessed=0, transcendentals=0),
    )(*args)


def flags(bits, lower, count):
    words = bits.shape[1]
    pieces = []
    at = lower
    while at < lower + count:
        flag, word = divmod(at, words)
        size = min(words - word, lower + count - at)
        pieces.append(lax.shift_right_logical(bits[:, word : word + size], flag) & 1)
        at += size
    return pieces[0] if len(pieces) == 1 else jnp.concatenate(pieces, axis=1)


def tile(frames, block, wanted, visible):
    frames_low = frames.astype(LOW)
    scaled = clipped_errors(frames_low, block, wanted, visible)
    return updated(frames_low, block, scaled), jnp.dot(
        scaled, block, preferred_element_type=jnp.float32
    )


def product(frames_low, block):
    return lax.dot_general(
        frames_low, block, (((1,), (1,)), ((), ())), preferred_element_type=jnp.float32
    )


def clipped_errors(frames_low, block, wanted, visible):
    return clipped_rest(product(frames_low, block), wanted, visible)


def clipped_rest(predicted, wanted, visible):
    errors = wanted.astype(jnp.float32) - predicted
    clipped = jnp.clip(errors, -1.0, 1.0)
    return jnp.where(visible != 0, clipped, 0.0).astype(LOW)


def updated(frames_low, block, scaled):
    grad_pixels = lax.dot_general(
        scaled, frames_low, (((0,), (0,)), ((), ())), preferred_element_type=jnp.float32
    )
    current = block.astype(jnp.float32)
    return (current + step_pixels * (grad_pixels - decay_weight * current)).astype(LOW)


def added(frames, done, grad):
    if done is None:
        return frames + step_frames * (grad - decay_weight * frames)
    return done + step_frames * grad


def body(observed, mask_bits, frame_factors, pixel_factors):
    width, rank = pixel_factors.shape
    rows = frame_factors.shape[0]
    visits = observed.shape[1] // width
    size = width // CHUNKS
    chunk_t = struct((size, rank))
    frames_t = struct((rows, rank), jnp.float32)
    early = 2 * size
    early_words = min(early, mask_bits.shape[1])

    def load_kernel(observed, mask_bits, frames_in, pixels_in, new, scaled, wanted, bits, frames, pixels, predicted, sems):
        @pl.when(is_odd())
        def _():
            copies = [
                pltpu.make_async_copy(frames_in, frames, sems.at[0]),
                pltpu.make_async_copy(pixels_in.at[:early], pixels, sems.at[1]),
                pltpu.make_async_copy(mask_bits.at[:, :early_words], bits, sems.at[2]),
                pltpu.make_async_copy(observed.at[:, :early], wanted, sems.at[3]),
            ]
            for copy in copies:
                copy.start(priority=1)
            for copy in copies[:2]:
                copy.wait()
            frames_low = frames[...].astype(LOW)
            predicted[...] = product(frames_low, pixels[...])
            for copy in copies[2:]:
                copy.wait()
            scaled[...] = clipped_rest(predicted[...], wanted[...], flags(bits, 0, early))
            new[:early] = updated(frames_low, pixels[...], scaled[...])

    new, scaled = call(
        "load",
        load_kernel,
        [
            pltpu.with_memory_space_constraint(a, pltpu.HBM)
            for a in (observed, mask_bits, frame_factors, pixel_factors)
        ],
        [struct((early + 16, rank)), struct((rows, early))],
        in_specs=[HBM] * 4,
        scratch=[
            pltpu.VMEM((rows, early), LOW),
            pltpu.VMEM((rows, early_words), mask_bits.dtype),
            pltpu.VMEM((rows, rank), jnp.float32),
            pltpu.VMEM((early, rank), LOW),
            pltpu.VMEM((rows, early), jnp.float32),
            DMA((4,)),
        ],
    )
    later, new = lax.optimization_barrier((observed, new))
    arrived = shifted(new, "blk")
    observed0, bits, pixels, frames = observed[:, :width], mask_bits, pixel_factors, frame_factors

    def middle_kernel(observed0, bits, pixels, frames, scaled, new0, new, done):
        end = early + size

        @pl.when(is_odd())
        def _():
            new[...], grad = tile(
                frames[...], pixels[early:end], observed0[:, early:end], flags(bits, early, size)
            )
            early_grad = jnp.dot(scaled[...], pixels[:early], preferred_element_type=jnp.float32)
            done[...] = added(frames[...], None, early_grad + grad)

        @pl.when(jnp.logical_not(is_odd()))
        def _():
            made, grad = tile(frames[...], pixels[:end], observed0[:, :end], flags(bits, 0, end))
            new0[...] = made[:early]
            new[...] = made[early:]
            done[...] = added(frames[...], None, grad)

    new0, new, done = call(
        "middle",
        middle_kernel,
        [observed0, bits, pixels, frames, scaled],
        [struct((early, rank)), chunk_t, frames_t],
    )
    third = shifted(new, "blk")
    handed = swapped(new0)
    coming = [None, None, third]

    def step(visit, chunk, block, frames, done, wanted):
        at = chunk * size
        first = done is None
        whole = visit == 0
        columns = visit * width + at

        split = isinstance(block, tuple)

        def kernel(wanted, bits, frames, *refs):
            if split:
                start = block[2]
                held = jnp.where(is_odd(), refs[1][...], refs[0][start : start + size])
                refs = refs[2:]
            else:
                held = refs[0][at : at + size] if whole else refs[0][...]
                refs = refs[1:]
            new, grad = tile(
                frames[...], held, wanted[:, columns : columns + size], flags(bits, visit * width + at, size)
            )
            refs[-2][...] = new
            refs[-1][...] = added(frames[...], None if first else refs[0][...], grad)

        blocks = list(block[:2]) if split else [block]
        args = [wanted, bits, frames, *blocks] + ([] if first else [done])
        return call(
            "step",
            kernel,
            args,
            [chunk_t, frames_t],
            aliases={} if first else {len(args) - 1: 1},
            flops=LAST_FLOPS if visit == visits - 1 else 0,
        )

    for c in range(3, CHUNKS):
        new, done = step(0, c, pixels, frames, done, observed0)
        coming.append(shifted(new, "blk"))

    def odd_kernel(wanted, bits, frames, block, new, done):
        @pl.when(is_odd())
        def _():
            new[...], grad = tile(
                frames[...], block[:size], wanted[:, width : width + size], flags(bits, width, size)
            )
            done[...] = added(frames[...], None, grad)

    def both_kernel(wanted, bits, frames, block, own, done, new0, new, done_out):
        @pl.when(is_odd())
        def _():
            at = width + size
            new[...], grad = tile(
                frames[...], own[size:], wanted[:, at : at + size], flags(bits, at, size)
            )
            done_out[...] = added(frames[...], done[...], grad)

        @pl.when(jnp.logical_not(is_odd()))
        def _():
            made, grad = tile(
                frames[...], block[:early], wanted[:, width : width + early], flags(bits, width, early)
            )
            new0[...] = made[:size]
            new[...] = made[size:]
            done_out[...] = added(frames[...], None, grad)

    def start_step(visit, block, frames):
        at = visit * width

        def kernel(wanted, bits, frames, block, new, scaled):
            frames_low = frames[...].astype(LOW)
            scaled[...] = clipped_errors(
                frames_low, block[...], wanted[:, at : at + size], flags(bits, at, size)
            )
            new[...] = updated(frames_low, block[...], scaled[...])

        return call(
            "start", kernel, [later, bits, frames, block], [chunk_t, struct((rows, size))]
        )

    def end_step(block, frames, scaled):
        def kernel(block, frames, scaled, done):
            grad = jnp.dot(scaled[...], block[...], preferred_element_type=jnp.float32)
            done[...] = added(frames[...], None, grad)

        return call("end", kernel, [block, frames, scaled], [frames_t])[0]

    frames = done
    new, done = call(
        "odd", odd_kernel, [later, bits, frames, handed], [chunk_t, frames_t]
    )
    passed = shifted(new, "blk")
    new0, new, done = call(
        "both",
        both_kernel,
        [later, bits, frames, arrived, handed, done],
        [chunk_t, chunk_t, frames_t],
        aliases={5: 2},
    )
    sent = [(passed, swapped(new0), 0), shifted(new, "blk")]
    for c in range(2, CHUNKS):
        new, done = step(1, c, coming[c], frames, done, later)
        sent.append(shifted(new, "blk"))
    coming = sent

    for visit in range(2, visits - 1):
        axis = "blk" if visit < visits - 2 else "wide"
        frames, done = done, None
        sent = []
        for c in range(CHUNKS):
            if c == 0 and visit == visits - 2:
                new, scaled = start_step(visit, coming[c], frames)
                sent.append(shifted(new, axis))
                done = end_step(coming[c], frames, scaled)
                continue
            new, done = step(visit, c, coming[c], frames, done, later)
            sent.append(shifted(new, axis))
        coming = sent

    frames, done = done, None
    visit = visits - 1
    written = None
    for c in range(CHUNKS - 1):
        new, done = step(visit, c, coming[c], frames, done, later)

        def write_kernel(new, *refs, at=c * size):
            pixels_out, sem = refs[-2:]
            copy = pltpu.make_async_copy(new, pixels_out.at[at : at + size], sem)
            copy.start()
            copy.wait()

        first = written is None
        written = call(
            "write",
            write_kernel,
            [new] if first else [new, written],
            [struct((width, rank))],
            in_specs=[VMEM] if first else [VMEM, HBM],
            out_specs=[HBM],
            scratch=[DMA],
            aliases={} if first else {1: 0},
            flops=LAST_FLOPS,
        )[0]

    def last_kernel(wanted, bits, block, frames, done, written, frames_out, pixels_out, new, sum_v, sems):
        del written
        at = width - size
        copies = [
            pltpu.make_async_copy(new, pixels_out.at[at:], sems.at[0]),
            pltpu.make_async_copy(sum_v, frames_out, sems.at[1]),
        ]
        columns = visit * width + at
        frames_low = frames[...].astype(LOW)
        scaled = clipped_errors(
            frames_low,
            block[...],
            wanted[:, columns : columns + size],
            flags(bits, visit * width + at, size),
        )
        grad = jnp.dot(scaled, block[...], preferred_element_type=jnp.float32)
        sum_v[...] = added(frames[...], done[...], grad)
        copies[-1].start(priority=1)
        new[...] = updated(frames_low, block[...], scaled)
        copies[0].start()
        for copy in copies:
            copy.wait()

    return call(
        "last",
        last_kernel,
        [later, bits, coming[-1], frames, done, written],
        [frames_t, struct((width, rank))],
        in_specs=[VMEM] * 5 + [HBM],
        out_specs=[HBM] * 2,
        aliases={5: 1},
        scratch=[pltpu.VMEM((size, rank), LOW), pltpu.VMEM((rows, rank), jnp.float32), DMA((2,))],
        flops=LAST_FLOPS,
    )


def solution(mesh):
    spec = P(("blk", "wide"), None)
    return jax.shard_map(
        body, mesh=mesh, in_specs=(spec,) * 4, out_specs=(spec, spec), check_vma=False
    )
```
